32 devices in a mesh: parts: 2 (over y), tile: 4 (over z), tm: 2 (over x), rep: 2 (over core).
Axes of the slice: x: 2, y: 2, z: 4, core: 2. Of those that a mesh axis runs over, the one named last changes fastest.
Arguments:
- probes: bfloat16 [128, 4, 8192], P(('parts', 'rep'), 'tm', 'tile'), parts along dimension 0, may hold values from -6 to 6
- footprints: bfloat16 [128, 128, 2048], P(('parts', 'tile', 'tm')), parts along dimension 0, may hold values from -0.25 to 0.25
- owner_tile: int32 [128, 1], P(('parts', 'tile', 'tm')), parts along dimension 0, may hold values from 0 to 3; in each aligned block of 8 rows (0 to 7, 8 to 15, ...) at most 2 rows name the same one
- sounding_index: int32 [128], P(('parts', 'tile', 'tm')), parts along dimension 0, may hold values from 0 to 1
- flux_step: int32 [128], P(('parts', 'tile', 'tm')), parts along dimension 0, may hold values from 0 to 1
- entry_count: int32 [16], P(('parts', 'tile', 'tm')), parts along dimension 0, may hold values from 1 to 8
- departure: float32 [16, 128], P(('parts', 'tile', 'tm')), parts along dimension 0, may hold values from -12 to 12
- live_count: int32 [16], P(('parts', 'tile', 'tm')), parts along dimension 0, may hold values from 32 to 128
- error_id: int32 [16], P(('parts', 'tile', 'tm')), parts along dimension 0, may hold values from 0 to 3
- precision_table: float32 [4, 128, 128], replicated, may hold values from -1 to 2, as said below
- temporal_factor: float32 [4, 4], replicated, may hold values from -3 to 3
- row_factor: float32 [16, 16], replicated, may hold values from -1.5 to 1.5
- column_factor: float32 [128, 128], replicated, may hold values from -0.5 to 0.5
Outputs:
- gradient: bfloat16 [128, 4, 8192], P(('parts', 'rep'), 'tm', 'tile'), parts along dimension 0
The draws below stay inside these ranges and needn't reach their ends.
There are 2 independent parts, one for each index of `parts`. The reference program is written for one: setup_inputs(seed, part) draws one part's arguments, and reference() takes and returns one part's arrays. A program takes and returns all parts, laid end to end along the dimension named above; an argument that names none is the same for every part. Nothing has to cross between parts.
Inputs may be any that keep to these rules, and one draw needn't show every extreme that they name: `owner_tile`: in the slots of one flux-holding device at most 2 name the same owner tile, and some device's slots reach 2. `precision_table`: each block is symmetric.
All inputs are finite; a program needn't handle non-finite values.
Results may differ from the reference program's by a relative error of at most 0.0061.
Values may be sent and summed in bfloat16 or wider, within the bound.
No kernel may reach another device: no remote copies, remote signals or barrier semaphores. Data moves between devices by JAX's collectives and lax.ppermute only.
A program may use at most 64 MiB of HBM per device.

```python
import math
import jax
import jax.numpy as jnp
import numpy as np
from jax import lax

PROBES = 64
T_DEV = 2
NT = 4
ROWS_B = 16
COLS_B = 128
FB = 2048
NS = 8192
SB = 128
SB_TILE = 2
NSB = 8
E_DEV = 8
HOLDERS = 8
E_TOTAL = 64
CAP = 2
NERR = 4
N_TILE = 4
N_TM = 2


def draw_entry_count(key, part):
    first, second, third, fourth = jax.random.split(jax.random.fold_in(key, 11), 4)
    high = jax.random.randint(first, (HOLDERS,), E_DEV - E_DEV // 4 - 1 + 1, E_DEV + 1)
    high = jnp.maximum(high, 1)
    low = jax.random.randint(second, (HOLDERS,), 1, E_DEV // 2 + 1)
    sparse = jax.random.randint(third, (HOLDERS,), 0, 8) == 0
    base = jnp.where(sparse, low, high)
    chosen = jax.random.randint(fourth, (), 0, HOLDERS)
    return base.at[chosen].set(E_DEV).astype(jnp.int32)


def draw_live_count(key, part):
    first, second = jax.random.split(jax.random.fold_in(key, 23), 2)
    counts = jax.random.randint(first, (NSB,), SB // 4, SB + 1)
    chosen = jax.random.randint(second, (), 0, NSB)
    return counts.at[chosen].set(SB).astype(jnp.int32)


def draw_precision_table(key, part):
    first, second = jax.random.split(jax.random.fold_in(key, 37), 2)
    noise = jax.random.uniform(first, (NERR, SB, SB), jnp.float32, -1.0, 1.0) / SB
    noise = 0.5 * (noise + jnp.swapaxes(noise, 1, 2))
    diagonal = jax.random.uniform(second, (NERR, SB), jnp.float32, 1.0, 2.0)
    eye = (jnp.arange(SB)[:, None] == jnp.arange(SB)[None, :]).astype(jnp.float32)
    return noise * (1.0 - eye)[None] + diagonal[:, :, None] * eye[None]


def plant(result, own_key, smallest, largest):
    shape = result.shape
    place = [jax.random.randint(jax.random.fold_in(own_key, axis), (), 0, shape[axis]) for axis in range(len(shape))]
    result = result.at[tuple(place)].set(smallest)
    longest = shape.index(max(shape))
    place[longest] = (place[longest] + 1) % shape[longest]
    return result.at[tuple(place)].set(largest)


def block_scale(key, extent, cuts, least, largest):
    def one(axis_at, parts):
        steps = jax.random.uniform(jax.random.fold_in(jax.random.fold_in(key, 6), axis_at), (parts,), jnp.float32, least / len(cuts), largest / len(cuts))
        return jnp.repeat(jnp.exp(steps), extent[axis_at] // parts).reshape((-1,) + (1,) * (len(extent) - axis_at - 1))

    gain = one(*cuts[0])
    for cut in cuts[1:]:
        gain = gain * one(*cut)
    return gain


def routed_block(stream_key, own, number, rows, amount, top, limit, skew):
    order = jax.random.permutation(stream_key, amount)
    heavy_load, usual = load_shares(amount, rows * top, limit, skew, True), load_shares(amount, rows * top, limit, skew, False)
    places = jnp.arange(amount)

    def named(lengths, rotation):
        used = int((lengths > 0).sum())
        fixed = max(1, used // 4)
        shifted = fixed + (places - fixed + rotation * (used - fixed)) % max(1, amount - fixed)
        return jnp.zeros((amount,), jnp.int32).at[order[jnp.where(places < fixed, places, shifted)]].set(jnp.asarray(lengths, jnp.int32))

    lengths = jnp.where(number % 4 == 0, named(heavy_load, number // 4), named(usual, number - number // 4 - 1))
    mixed = jax.random.permutation(jax.random.fold_in(own, 3), amount)
    donor, sink = mixed[0:amount // 2 * 2:2], mixed[1:amount // 2 * 2:2]
    slack = jnp.minimum(lengths[donor] - 1, limit - lengths[sink]) // 2
    slack = jnp.where((donor == order[0]) | (sink == order[0]) | (lengths[sink] == 0), 0, jnp.maximum(slack, 0))
    shifted = jax.random.randint(jax.random.fold_in(own, 4), (amount // 2,), 0, 1 << 20) % (slack + 1)
    lengths = lengths.at[donor].add(-shifted).at[sink].add(shifted)
    labels = jnp.searchsorted(jnp.cumsum(lengths), jnp.arange(rows * top), side="right").astype(jnp.int32)
    table = labels.reshape(top, rows).T
    table = table[jax.random.permutation(jax.random.fold_in(own, 1), rows)]
    rotation = jax.random.randint(jax.random.fold_in(own, 2), (rows, 1), 0, top)
    return jnp.take_along_axis(table, (jnp.arange(top)[None, :] + rotation) % top, axis=1)


def load_shares(number_of, total, reach, slope, full):
    portions = [(1 << 20) // math.isqrt(grade ** slope) + 1 for grade in range(1, number_of + 1)]
    largest = reach if full else min(reach, max(-(-total // number_of), total * portions[0] // sum(portions)))
    least = 1 if total - largest >= number_of - 1 else 0
    holding, surplus = [largest] + [least] * (number_of - 1), total - largest - least * (number_of - 1)
    while surplus > 0:
        free = [i for i in range(1, number_of) if holding[i] < largest] or [i for i in range(1, number_of) if holding[i] < reach]
        mass, left = sum([portions[i] for i in free]), surplus
        for i in free:
            more = min(reach - holding[i], max(1, left * portions[i] // mass), surplus)
            holding[i] = holding[i] + more
            surplus = surplus - more
    return np.array(holding)


def bell_draw(own_key, dims, spread, bound, shards=(), held_as=jnp.bfloat16):
    level = block_scale(own_key, dims, shards, -0.22, 0.18) if shards else 1.0
    array = jax.random.normal(own_key, dims, jnp.float32) * spread * level
    return jnp.minimum(jnp.maximum(array, -bound), bound).astype(held_as)


def setup_inputs(seed: int = 0, part: int = 0) -> dict:
    arg_keys = jax.random.split(jax.random.key(seed), 14)
    part_splits = jax.random.split(jax.random.fold_in(arg_keys[13], part), 14)
    probes = bell_draw(part_splits[0], (PROBES, NT, NS), 1.0, 6.0, ((0, 2), (1, 2), (2, 4)))
    footprints = bell_draw(part_splits[1], (E_TOTAL, SB, FB), (FB // 4) ** -0.5, 0.25, ((0, 8),))
    owner_tile_keys = jax.random.split(jax.random.fold_in(part_splits[2], 1), E_TOTAL // E_DEV)
    owner_tile_turns = jax.random.permutation(jax.random.fold_in(part_splits[2], 3), E_TOTAL // E_DEV)
    owner_tile = jax.vmap(lambda own, number: routed_block(jax.random.fold_in(part_splits[2], 2), own, number, E_DEV, N_TILE, 1, CAP, 2))(owner_tile_keys, owner_tile_turns).reshape((E_TOTAL, 1))
    sounding_index = plant(jax.random.randint(part_splits[3], (E_TOTAL,), 0, SB_TILE), jax.random.fold_in(part_splits[3], 1), 0, SB_TILE - 1).astype(jnp.int32)
    flux_step = plant(jax.random.randint(part_splits[4], (E_TOTAL,), 0, T_DEV), jax.random.fold_in(part_splits[4], 1), 0, T_DEV - 1).astype(jnp.int32)
    entry_count = draw_entry_count(jax.random.fold_in(jax.random.fold_in(arg_keys[13], part), 71), part)
    departure = bell_draw(part_splits[6], (NSB, SB), 2.0, 12.0, ((0, 8),), jnp.float32)
    live_count = draw_live_count(jax.random.fold_in(jax.random.fold_in(arg_keys[13], part), 71), part)
    error_id = plant(jax.random.randint(part_splits[8], (NSB,), 0, NERR), jax.random.fold_in(part_splits[8], 1), 0, NERR - 1).astype(jnp.int32)
    precision_table = draw_precision_table(jax.random.fold_in(arg_keys[13], 71), part)
    temporal_factor = bell_draw(arg_keys[10], (NT, NT), NT ** -0.5, 3.0, (), jnp.float32)
    row_factor = bell_draw(arg_keys[11], (ROWS_B, ROWS_B), ROWS_B ** -0.5, 1.5, (), jnp.float32)
    column_factor = bell_draw(arg_keys[12], (COLS_B, COLS_B), COLS_B ** -0.5, 0.5, (), jnp.float32)
    return dict(probes=probes, footprints=footprints, owner_tile=owner_tile, sounding_index=sounding_index, flux_step=flux_step, entry_count=entry_count, departure=departure, live_count=live_count, error_id=error_id, precision_table=precision_table, temporal_factor=temporal_factor, row_factor=row_factor, column_factor=column_factor)


def spatial_forward(field, row_factor, column_factor):
    patch = field.reshape(PROBES, NT, N_TILE, ROWS_B, COLS_B)
    patch = jnp.einsum("ij,ptnjc->ptnic", row_factor, patch, precision=lax.Precision.HIGHEST)
    patch = jnp.einsum("ptnic,kc->ptnik", patch, column_factor, precision=lax.Precision.HIGHEST)
    return patch.reshape(PROBES, NT, NS)


def spatial_adjoint(field, row_factor, column_factor):
    patch = field.reshape(PROBES, NT, N_TILE, ROWS_B, COLS_B)
    patch = jnp.einsum("ij,ptnic->ptnjc", row_factor, patch, precision=lax.Precision.HIGHEST)
    patch = jnp.einsum("ptnjc,ck->ptnjk", patch, column_factor, precision=lax.Precision.HIGHEST)
    return patch.reshape(PROBES, NT, NS)


def reference(probes, footprints, owner_tile, sounding_index, flux_step, entry_count, departure, live_count, error_id, precision_table, temporal_factor, row_factor, column_factor):
    highest = lax.Precision.HIGHEST
    mixed = jnp.einsum("tk,pks->pts", temporal_factor, probes.astype(jnp.float32), precision=highest)
    fluxes = spatial_forward(mixed, row_factor, column_factor).astype(jnp.bfloat16)
    entry = jnp.arange(E_TOTAL, dtype=jnp.int32)
    holder = entry // E_DEV
    tiles = (holder // N_TM).astype(jnp.int32)
    times = ((holder % N_TM) * T_DEV + flux_step).astype(jnp.int32)
    live = ((entry % E_DEV) < entry_count[holder]).astype(jnp.float32)
    target = (owner_tile[:, 0] * SB_TILE + sounding_index).astype(jnp.int32)

    def forward(total, item):
        footprint, time, tile, alive, block = item
        piece = lax.dynamic_slice(fluxes, (jnp.int32(0), time, tile * FB), (PROBES, 1, FB))[:, 0, :]
        part = lax.dot_general(piece, footprint, (((1,), (1,)), ((), ())), preferred_element_type=jnp.float32) * alive
        current = lax.dynamic_index_in_dim(total, block, 0, keepdims=False)
        return lax.dynamic_update_index_in_dim(total, current + part, block, 0), None

    predictions, _ = lax.scan(forward, jnp.zeros((NSB, PROBES, SB), jnp.float32), (footprints, times, tiles, live, target))
    mask = (jnp.arange(SB, dtype=jnp.int32)[None, :] < live_count[:, None]).astype(jnp.float32)
    residual = (predictions - departure[:, None, :]) * mask[:, None, :]
    precision = precision_table[error_id]
    weights = (jnp.einsum("bps,bsk->bpk", residual, precision, precision=highest) * mask[:, None, :]).astype(jnp.bfloat16)

    def backward(total, item):
        footprint, time, tile, alive, block = item
        weight = lax.dynamic_index_in_dim(weights, block, 0, keepdims=False)
        term = jnp.dot(weight, footprint, preferred_element_type=jnp.float32) * alive
        start = (jnp.int32(0), time, tile * FB)
        current = lax.dynamic_slice(total, start, (PROBES, 1, FB))
        return lax.dynamic_update_slice(total, current + term[:, None, :], start), None

    adjoint, _ = lax.scan(backward, jnp.zeros((PROBES, NT, NS), jnp.float32), (footprints, times, tiles, live, target))
    back = spatial_adjoint(adjoint, row_factor, column_factor).astype(jnp.bfloat16)
    pulled = jnp.einsum("tk,pts->pks", temporal_factor, back.astype(jnp.float32), precision=highest)
    return (probes.astype(jnp.float32) + pulled).astype(jnp.bfloat16)
```

```python
import functools

import jax
import jax.numpy as jnp
from jax import lax
from jax.experimental import pallas as pl
from jax.experimental.pallas import tpu as pltpu
from jax.sharding import PartitionSpec as P

F32 = jnp.float32
BF16 = jnp.bfloat16
LANES = 128
VMEM_LIMIT = 12 * 1024 * 1024

in_vmem = pl.BlockSpec(memory_space=pltpu.VMEM)
in_hbm = pl.BlockSpec(memory_space=pltpu.HBM)
in_smem = pl.BlockSpec(memory_space=pltpu.SMEM)


def halves(value):
    high = value.astype(BF16)
    low = (value - high.astype(F32)).astype(BF16)
    return high, low


def widen(value):
    high, low = halves(value)
    return jnp.concatenate(
        [
            jnp.concatenate([high, low], axis=1),
            jnp.concatenate([high, jnp.zeros_like(low)], axis=1),
        ],
        axis=0,
    )


def times_wide(value, wide):
    high, low = halves(value)
    both = jnp.dot(
        jnp.concatenate([high, low], axis=1), wide, preferred_element_type=F32
    )
    size = both.shape[1] // 2
    return both[:, :size] + both[:, size:]


def mixing(factor, group, groups, steps, count, forward):
    block = steps * count
    row = lax.broadcasted_iota(jnp.int32, (block, groups * block), 0)
    col = lax.broadcasted_iota(jnp.int32, (block, groups * block), 1)
    peer, within = lax.div(col, block), lax.rem(col, block)
    if forward:
        row_step, row_probe = lax.div(row, count), lax.rem(row, count)
        col_probe, col_step = lax.div(within, steps), lax.rem(within, steps)
    else:
        row_probe, row_step = lax.div(row, steps), lax.rem(row, steps)
        col_step, col_probe = lax.div(within, count), lax.rem(within, count)
    value = jnp.zeros((block, groups * block), F32)
    same = row_probe == col_probe
    for other in range(groups):
        for a in range(steps):
            for b in range(steps):
                mine, theirs = group * steps + a, (group ^ other) * steps + b
                scale = factor[mine, theirs] if forward else factor[theirs, mine]
                here = same & (peer == other) & (row_step == a) & (col_step == b)
                value = jnp.where(here, scale, value)
    return jnp.concatenate(halves(value), axis=0)


def prepare_kernel(
    groups, steps, count, blocks, own_blocks,
    footprints, table, temporal, row_factor, column, owner, sounding, flux_step,
    departure, entries, live_count, error_id,
    held, table_at, rows_at, mix_f, mix_b, wide_f, wide_b, base, place, step_of,
    factor, column_at, owner_at, sounding_at, flux_at, departure_at, sems,
):
    pairs = [
        (temporal, factor), (column, column_at), (departure, departure_at), (owner, owner_at),
        (sounding, sounding_at), (flux_step, flux_at), (row_factor, rows_at),
        (table, table_at), (footprints, held),
    ]
    copies = [pltpu.make_async_copy(a, b, sems.at[n]) for n, (a, b) in enumerate(pairs)]
    for copy in copies:
        copy.start()
    for copy in copies[:-2]:
        copy.wait()
    group = lax.axis_index("tm")
    mix_f[...] = mixing(factor, group, groups, steps, count, True)
    mix_b[...] = mixing(factor, group, groups, steps, count, False)
    wide_f[...] = widen(column_at[...].T)
    wide_b[...] = widen(column_at[...])
    base[...] = jnp.zeros_like(base)
    block_rows = base.shape[1]
    for q in range(own_blocks):
        at = (lax.axis_index("tile") * groups + group) * own_blocks + q
        base[pl.ds(pl.multiple_of(at * count, count), count), :] = jnp.broadcast_to(
            -departure_at[q : q + 1, :], (count, block_rows)
        )
        base[pl.ds(blocks * count + at, 1), :] = jnp.full(
            (1, block_rows), live_count[q].astype(F32)
        )
        base[pl.ds(blocks * count + blocks + at, 1), :] = jnp.full(
            (1, block_rows), error_id[q].astype(F32)
        )
    for e in range(place.shape[0]):
        place[e] = owner_at[e] * (groups * own_blocks) + sounding_at[e]
        step_of[e] = jnp.where(e < entries[0], flux_at[e], steps)
    for copy in copies[-2:]:
        copy.wait()


def row_mix(field, row_factor, transposed, wide, place):
    rows = row_factor.shape[0]
    batch = 4
    for start in range(0, rows, batch):
        sums = [None] * batch
        for j in range(rows):
            tile = field[:, j * LANES : (j + 1) * LANES]
            for n in range(batch):
                i = start + n
                scale = row_factor[j, i] if transposed else row_factor[i, j]
                term = scale * tile
                sums[n] = term if sums[n] is None else sums[n] + term
        result = times_wide(jnp.concatenate(sums, axis=0), wide).astype(BF16)
        size = sums[0].shape[0]
        for n in range(batch):
            i = start + n
            place[:, i * LANES : (i + 1) * LANES] = result[n * size : (n + 1) * size]


def predict_kernel(groups, steps, count, *refs):
    fields = refs[:groups]
    (
        mix_f, row_factor, wide_f, held, base, place, step_of, total,
        mixed, fluxes,
    ) = refs[groups:]
    slots = place.shape[0]
    block_rows = base.shape[1]
    stacked = jnp.concatenate(
        [fields[0][...]] + [f[...].reshape(fields[0].shape) for f in fields[1:]], axis=0
    )
    both = jnp.dot(mix_f[...], stacked, preferred_element_type=F32)
    size = steps * count
    mixed[...] = both[:size] + both[size:]
    row_mix(mixed, row_factor, False, wide_f[...], fluxes)
    total[...] = base[...]
    flux = fluxes[...]
    for e in range(slots):
        part = lax.dot_general(
            flux,
            held[e * block_rows : (e + 1) * block_rows, :],
            (((1,), (1,)), ((), ())),
            preferred_element_type=F32,
        )
        chosen = jnp.zeros((count, block_rows), F32)
        for t in range(steps):
            chosen = jnp.where(step_of[e] == t, part[t * count : (t + 1) * count], chosen)
        at = pl.ds(pl.multiple_of(place[e] * count, count), count)
        total[at, :] = total[at, :] + chosen


def adjoint_kernel(
    steps, count, blocks,
    total, table, row_factor, wide_b, held, place, step_of,
    back, weights, adjoint,
):
    block_rows = table.shape[1]
    slots = place.shape[0]
    lane = lax.broadcasted_iota(jnp.int32, (1, block_rows), 1).astype(F32)
    for e in range(slots):
        target = place[e]
        live = total[pl.ds(blocks * count + target, 1), :]
        error = total[pl.ds(blocks * count + blocks + target, 1), :]
        mask = jnp.where(lane < live, 1.0, 0.0)
        residual = total[pl.ds(pl.multiple_of(target * count, count), count), :] * mask
        precision = table[0]
        for n in range(1, table.shape[0]):
            precision = jnp.where(error == n, table[n], precision)
        weight = times_wide(residual, widen(precision)) * mask
        for t in range(steps):
            weights[t * count : (t + 1) * count, e * block_rows : (e + 1) * block_rows] = (
                jnp.where(step_of[e] == t, weight, 0.0).astype(BF16)
            )
    adjoint[...] = jnp.dot(weights[...], held[...], preferred_element_type=F32)
    row_mix(adjoint, row_factor, True, wide_b[...], back)


def finish_kernel(groups, *refs):
    backs = refs[:groups]
    probes, mix_b, out = refs[groups:]
    stacked = jnp.concatenate([b[...] for b in backs], axis=0)
    both = jnp.dot(mix_b[...], stacked, preferred_element_type=F32)
    size = out.shape[0]
    out[...] = (probes[...].astype(F32) + (both[:size] + both[size:])).astype(BF16)


def exchange(value, axis, distance):
    size = lax.axis_size(axis)
    return lax.ppermute(value, axis, [(i, i ^ distance) for i in range(size)])


def subsets(spans):
    choices = [[]]
    for span in spans:
        choices = choices + [c + [span] for c in choices]
    return choices[:0:-1]


def hop(value, moves):
    tiles, groups = lax.axis_size("tile"), lax.axis_size("tm")
    flip = sum(d * groups if axis == "tile" else d for axis, d in moves)
    return lax.ppermute(
        value, ("tile", "tm"), [(i, i ^ flip) for i in range(tiles * groups)]
    )


def everywhere(value):
    spans = [
        (axis, 1 << n)
        for axis in ("tm", "tile")
        for n in range(lax.axis_size(axis).bit_length() - 1)
    ]
    for start in range(0, len(spans), 2):
        sent = value.astype(BF16)
        terms = [hop(sent, moves) for moves in subsets(spans[start : start + 2])]
        for term in terms:
            value = value + term.astype(F32)
    return value


def outside(*values):
    return [pltpu.with_memory_space_constraint(x, pltpu.HBM) for x in values]


def per_device(
    probes,
    footprints,
    owner_tile,
    sounding_index,
    flux_step,
    entry_count,
    departure,
    live_count,
    error_id,
    precision_table,
    temporal_factor,
    row_factor,
    column_factor,
):
    count, steps, cells = probes.shape
    slots, block_rows = footprints.shape[:2]
    groups = lax.axis_size("tm")
    own_blocks = departure.shape[0]
    blocks = own_blocks * groups * lax.axis_size("tile")
    size = steps * count
    params = pltpu.CompilerParams(vmem_limit_bytes=VMEM_LIMIT)

    peers = [exchange(probes, "tm", d) for d in range(1, groups)]
    own = probes.reshape(size, cells)
    held, table, rows, mix_f, mix_b, wide_f, wide_b, base, place, step_of = pl.pallas_call(
        functools.partial(prepare_kernel, groups, steps, count, blocks, own_blocks),
        out_shape=[
            pltpu.VMEM((slots * block_rows, cells), BF16),
            pltpu.VMEM(precision_table.shape, F32),
            pltpu.SMEM(row_factor.shape, F32),
            pltpu.VMEM((2 * size, groups * size), BF16),
            pltpu.VMEM((2 * size, groups * size), BF16),
            pltpu.VMEM((2 * LANES, 2 * LANES), BF16),
            pltpu.VMEM((2 * LANES, 2 * LANES), BF16),
            pltpu.VMEM((blocks * (count + 2), block_rows), F32),
            pltpu.SMEM((slots,), jnp.int32),
            pltpu.SMEM((slots,), jnp.int32),
        ],
        in_specs=[in_hbm] * 9 + [in_smem] * 3,
        out_specs=[in_vmem] * 2 + [in_smem] + [in_vmem] * 5 + [in_smem] * 2,
        scratch_shapes=[
            pltpu.SMEM(temporal_factor.shape, F32),
            pltpu.VMEM(column_factor.shape, F32),
            pltpu.SMEM((slots,), jnp.int32),
            pltpu.SMEM((slots,), jnp.int32),
            pltpu.SMEM((slots,), jnp.int32),
            pltpu.VMEM(departure.shape, F32),
            pltpu.SemaphoreType.DMA((9,)),
        ],
        compiler_params=params,
        name="prepare",
    )(
        *outside(
            footprints.reshape(slots * block_rows, cells), precision_table, temporal_factor, row_factor, column_factor,
            owner_tile.reshape(slots), sounding_index, flux_step, departure,
        ),
        entry_count, live_count, error_id,
    )
    held, table, mix_f, mix_b, wide_f, wide_b, base = [
        pltpu.with_memory_space_constraint(x, pltpu.VMEM)
        for x in (held, table, mix_f, mix_b, wide_f, wide_b, base)
    ]

    total = pl.pallas_call(
        functools.partial(predict_kernel, groups, steps, count),
        out_shape=jax.ShapeDtypeStruct(base.shape, F32),
        in_specs=[in_vmem] * (groups + 1) + [in_smem] + [in_vmem] * 3 + [in_smem] * 2,
        out_specs=in_vmem,
        scratch_shapes=[
            pltpu.VMEM((size, cells), F32),
            pltpu.VMEM((size, cells), BF16),
        ],
        compiler_params=params,
        name="predict",
    )(
        own, *peers,
        mix_f, rows, wide_f, held, base, place, step_of,
    )
    total = everywhere(total)

    back = pl.pallas_call(
        functools.partial(adjoint_kernel, steps, count, blocks),
        out_shape=jax.ShapeDtypeStruct((size, cells), BF16),
        in_specs=[in_vmem] * 2 + [in_smem] + [in_vmem] * 2 + [in_smem] * 2,
        out_specs=in_vmem,
        scratch_shapes=[
            pltpu.VMEM((size, slots * block_rows), BF16),
            pltpu.VMEM((size, cells), F32),
        ],
        compiler_params=params,
        name="adjoint",
    )(total, table, rows, wide_b, held, place, step_of)

    backs = [back] + [exchange(back, "tm", d) for d in range(1, groups)]
    result = pl.pallas_call(
        functools.partial(finish_kernel, groups),
        out_shape=jax.ShapeDtypeStruct((size, cells), BF16),
        in_specs=[in_vmem] * (groups + 2),
        out_specs=in_vmem,
        compiler_params=params,
        name="finish",
    )(*backs, own, mix_b)
    return result.reshape(count, steps, cells)


def solution(mesh):
    placed = (
        P(("parts", "rep"), "tm", "tile"),
        P(("parts", "tile", "tm"), None, None),
        P(("parts", "tile", "tm"), None),
        P(("parts", "tile", "tm")),
        P(("parts", "tile", "tm")),
        P(("parts", "tile", "tm")),
        P(("parts", "tile", "tm"), None),
        P(("parts", "tile", "tm")),
        P(("parts", "tile", "tm")),
        P(),
        P(),
        P(),
        P(),
    )
    return jax.shard_map(
        per_device,
        mesh=mesh,
        in_specs=placed,
        out_specs=P(("parts", "rep"), "tm", "tile"),
        check_vma=False,
    )
```

```python
import functools

import jax
import jax.numpy as jnp
from jax import lax
from jax.experimental import pallas as pl
from jax.experimental.pallas import tpu as pltpu
from jax.sharding import PartitionSpec as P

F32 = jnp.float32
BF16 = jnp.bfloat16
LANES = 128
VMEM_LIMIT = 12 * 1024 * 1024

in_vmem = pl.BlockSpec(memory_space=pltpu.VMEM)
in_hbm = pl.BlockSpec(memory_space=pltpu.HBM)
in_smem = pl.BlockSpec(memory_space=pltpu.SMEM)


def halves(value):
    high = value.astype(BF16)
    low = (value - high.astype(F32)).astype(BF16)
    return high, low


def widen(value):
    high, low = halves(value)
    return jnp.concatenate(
        [
            jnp.concatenate([high, low], axis=1),
            jnp.concatenate([high, jnp.zeros_like(low)], axis=1),
        ],
        axis=0,
    )


def times_wide(value, wide):
    high, low = halves(value)
    both = jnp.dot(
        jnp.concatenate([high, low], axis=1), wide, preferred_element_type=F32
    )
    size = both.shape[1] // 2
    return both[:, :size] + both[:, size:]


def mixing(factor, group, groups, steps, count, forward):
    block = steps * count
    row = lax.broadcasted_iota(jnp.int32, (block, groups * block), 0)
    col = lax.broadcasted_iota(jnp.int32, (block, groups * block), 1)
    peer, within = lax.div(col, block), lax.rem(col, block)
    if forward:
        row_step, row_probe = lax.div(row, count), lax.rem(row, count)
        col_probe, col_step = lax.div(within, steps), lax.rem(within, steps)
    else:
        row_probe, row_step = lax.div(row, steps), lax.rem(row, steps)
        col_step, col_probe = lax.div(within, count), lax.rem(within, count)
    value = jnp.zeros((block, groups * block), F32)
    same = row_probe == col_probe
    for other in range(groups):
        for a in range(steps):
            for b in range(steps):
                mine, theirs = group * steps + a, (group ^ other) * steps + b
                scale = factor[mine, theirs] if forward else factor[theirs, mine]
                here = same & (peer == other) & (row_step == a) & (col_step == b)
                value = jnp.where(here, scale, value)
    return jnp.concatenate(halves(value), axis=0)


def prepare_kernel(
    groups, steps, count, blocks, own_blocks,
    footprints, probes, table, temporal, row_factor, column, owner, sounding, flux_step,
    departure, counts,
    held, turned, own, table_at, rows_at, mix_f, mix_b, wide_f, wide_b, base, place, step_of,
    factor, column_at, owner_at, sounding_at, flux_at, departure_at, counts_at,
    sems, held_sems,
):
    slots = place.shape[0]
    block_rows = base.shape[1]
    pairs = [
        (temporal, factor), (column, column_at), (departure, departure_at), (owner, owner_at),
        (sounding, sounding_at), (flux_step, flux_at), (counts, counts_at), (row_factor, rows_at),
        (table, table_at), (probes, own),
    ]
    copies = [pltpu.make_async_copy(a, b, sems.at[n]) for n, (a, b) in enumerate(pairs)]
    fetches = []
    for e in range(slots):
        rows = pl.ds(e * block_rows, block_rows)
        fetches.append(
            pltpu.make_async_copy(footprints.at[rows], held.at[rows], held_sems.at[e])
        )
    for copy in copies + fetches:
        copy.start()
    for copy in copies:
        copy.wait()
    group = lax.axis_index("tm")
    mix_f[...] = mixing(factor, group, groups, steps, count, True)
    mix_b[...] = mixing(factor, group, groups, steps, count, False)
    wide_f[...] = widen(column_at[...].T)
    wide_b[...] = widen(column_at[...])
    base[...] = jnp.zeros_like(base)
    for q in range(own_blocks):
        at = (lax.axis_index("tile") * groups + group) * own_blocks + q
        base[pl.ds(pl.multiple_of(at * count, count), count), :] = jnp.broadcast_to(
            -departure_at[q : q + 1, :], (count, block_rows)
        )
        base[pl.ds(blocks * count + at, 1), :] = jnp.full(
            (1, block_rows), counts_at[1 + q].astype(F32)
        )
        base[pl.ds(blocks * count + blocks + at, 1), :] = jnp.full(
            (1, block_rows), counts_at[1 + own_blocks + q].astype(F32)
        )
    for e in range(slots):
        place[e] = owner_at[e] * (groups * own_blocks) + sounding_at[e]
        step_of[e] = jnp.where(e < counts_at[0], flux_at[e], steps)
    for e in range(slots):
        fetches[e].wait()
        turned[:, e * block_rows : (e + 1) * block_rows] = held[
            e * block_rows : (e + 1) * block_rows, :
        ].T


def row_mix(field, row_factor, transposed, wide, place):
    rows = row_factor.shape[0]
    batch = 4
    for start in range(0, rows, batch):
        sums = [None] * batch
        for j in range(rows):
            tile = field[:, j * LANES : (j + 1) * LANES]
            for n in range(batch):
                i = start + n
                scale = row_factor[j, i] if transposed else row_factor[i, j]
                term = scale * tile
                sums[n] = term if sums[n] is None else sums[n] + term
        result = times_wide(jnp.concatenate(sums, axis=0), wide).astype(BF16)
        size = sums[0].shape[0]
        for n in range(batch):
            i = start + n
            place[:, i * LANES : (i + 1) * LANES] = result[n * size : (n + 1) * size]


def predict_kernel(groups, steps, count, *refs):
    fields = refs[:groups]
    mix_f, row_factor, wide_f, turned, base, place, step_of, total, mixed, fluxes = refs[groups:]
    block_rows = base.shape[1]
    stacked = jnp.concatenate([f[...].reshape(mixed.shape) for f in fields], axis=0)
    both = jnp.dot(mix_f[...], stacked, preferred_element_type=F32)
    size = steps * count
    mixed[...] = both[:size] + both[size:]
    row_mix(mixed, row_factor, False, wide_f[...], fluxes)
    total[...] = base[...]
    parts = jnp.dot(fluxes[...], turned[...], preferred_element_type=F32)
    for e in range(place.shape[0]):
        part = parts[:, e * block_rows : (e + 1) * block_rows]
        chosen = jnp.zeros((count, block_rows), F32)
        for t in range(steps):
            chosen = jnp.where(step_of[e] == t, part[t * count : (t + 1) * count], chosen)
        at = pl.ds(pl.multiple_of(place[e] * count, count), count)
        total[at, :] = total[at, :] + chosen


def adjoint_kernel(
    steps, count, blocks,
    total, table, row_factor, wide_b, held, place, step_of,
    back, weights, adjoint,
):
    block_rows = table.shape[1]
    slots = place.shape[0]
    lane = lax.broadcasted_iota(jnp.int32, (1, block_rows), 1).astype(F32)
    for e in range(slots):
        target = place[e]
        live = total[pl.ds(blocks * count + target, 1), :]
        error = total[pl.ds(blocks * count + blocks + target, 1), :]
        mask = jnp.where(lane < live, 1.0, 0.0)
        residual = total[pl.ds(pl.multiple_of(target * count, count), count), :] * mask
        precision = table[0]
        for n in range(1, table.shape[0]):
            precision = jnp.where(error == n, table[n], precision)
        weight = times_wide(residual, widen(precision)) * mask
        for t in range(steps):
            weights[t * count : (t + 1) * count, e * block_rows : (e + 1) * block_rows] = (
                jnp.where(step_of[e] == t, weight, 0.0).astype(BF16)
            )
    adjoint[...] = jnp.dot(weights[...], held[...], preferred_element_type=F32)
    row_mix(adjoint, row_factor, True, wide_b[...], back)


def finish_kernel(groups, *refs):
    backs = refs[:groups]
    probes, mix_b, out = refs[groups:]
    stacked = jnp.concatenate([b[...] for b in backs], axis=0)
    both = jnp.dot(mix_b[...], stacked, preferred_element_type=F32)
    size = both.shape[0] // 2
    before = probes[...].reshape(size, both.shape[1]).astype(F32)
    after = (before + (both[:size] + both[size:])).astype(BF16)
    out[...] = after.reshape(out.shape)


def exchange(value, axis, distance):
    size = lax.axis_size(axis)
    return lax.ppermute(value, axis, [(i, i ^ distance) for i in range(size)])


def subsets(spans):
    choices = [[]]
    for span in spans:
        choices = choices + [c + [span] for c in choices]
    return choices[1:]


def hop(value, moves):
    tiles, groups = lax.axis_size("tile"), lax.axis_size("tm")
    flip = sum(d * groups if axis == "tile" else d for axis, d in moves)
    return lax.ppermute(
        value, ("tile", "tm"), [(i, i ^ flip) for i in range(tiles * groups)]
    )


def everywhere(value):
    spans = [
        (axis, 1 << n)
        for axis in ("tm", "tile")
        for n in range(lax.axis_size(axis).bit_length() - 1)
    ]
    for start in range(0, len(spans), 2):
        sent = value.astype(BF16)
        terms = [hop(sent, moves) for moves in subsets(spans[start : start + 2])]
        for term in terms:
            value = value + term.astype(F32)
    return value


def outside(*values):
    return [pltpu.with_memory_space_constraint(x, pltpu.HBM) for x in values]


def inside(*values):
    return [pltpu.with_memory_space_constraint(x, pltpu.VMEM) for x in values]


def per_device(
    probes,
    footprints,
    owner_tile,
    sounding_index,
    flux_step,
    entry_count,
    departure,
    live_count,
    error_id,
    precision_table,
    temporal_factor,
    row_factor,
    column_factor,
):
    count, steps, cells = probes.shape
    slots, block_rows = footprints.shape[:2]
    groups = lax.axis_size("tm")
    own_blocks = departure.shape[0]
    blocks = own_blocks * groups * lax.axis_size("tile")
    size = steps * count
    params = pltpu.CompilerParams(vmem_limit_bytes=VMEM_LIMIT)

    peers = [exchange(probes, "tm", d) for d in range(1, groups)]
    held, turned, own, table, rows, mix_f, mix_b, wide_f, wide_b, base, place, step_of = (
        pl.pallas_call(
            functools.partial(prepare_kernel, groups, steps, count, blocks, own_blocks),
            out_shape=[
                pltpu.VMEM((slots * block_rows, cells), BF16),
                pltpu.VMEM((cells, slots * block_rows), BF16),
                pltpu.VMEM(probes.shape, BF16),
                pltpu.VMEM(precision_table.shape, F32),
                pltpu.SMEM(row_factor.shape, F32),
                pltpu.VMEM((2 * size, groups * size), BF16),
                pltpu.VMEM((2 * size, groups * size), BF16),
                pltpu.VMEM((2 * LANES, 2 * LANES), BF16),
                pltpu.VMEM((2 * LANES, 2 * LANES), BF16),
                pltpu.VMEM((blocks * (count + 2), block_rows), F32),
                pltpu.SMEM((slots,), jnp.int32),
                pltpu.SMEM((slots,), jnp.int32),
            ],
            in_specs=[in_hbm] * 11,
            out_specs=[in_vmem] * 4 + [in_smem] + [in_vmem] * 5 + [in_smem] * 2,
            scratch_shapes=[
                pltpu.SMEM(temporal_factor.shape, F32),
                pltpu.VMEM(column_factor.shape, F32),
                pltpu.SMEM((slots,), jnp.int32),
                pltpu.SMEM((slots,), jnp.int32),
                pltpu.SMEM((slots,), jnp.int32),
                pltpu.VMEM(departure.shape, F32),
                pltpu.SMEM((1 + 2 * own_blocks,), jnp.int32),
                pltpu.SemaphoreType.DMA((10,)),
                pltpu.SemaphoreType.DMA((slots,)),
            ],
            compiler_params=params,
            name="prepare",
        )(
            *outside(
                footprints.reshape(slots * block_rows, cells), probes, precision_table,
                temporal_factor, row_factor, column_factor, owner_tile.reshape(slots),
                sounding_index, flux_step, departure,
            ),
            jnp.concatenate([entry_count, live_count, error_id]),
        )
    )
    held, turned, own, table, mix_f, mix_b, wide_f, wide_b, base = inside(
        held, turned, own, table, mix_f, mix_b, wide_f, wide_b, base
    )

    total = pl.pallas_call(
        functools.partial(predict_kernel, groups, steps, count),
        out_shape=jax.ShapeDtypeStruct(base.shape, F32),
        in_specs=[in_vmem] * (groups + 1) + [in_smem] + [in_vmem] * 3 + [in_smem] * 2,
        out_specs=in_vmem,
        scratch_shapes=[
            pltpu.VMEM((size, cells), F32),
            pltpu.VMEM((size, cells), BF16),
        ],
        compiler_params=params,
        name="predict",
    )(own, *peers, mix_f, rows, wide_f, turned, base, place, step_of)
    total = everywhere(total)

    back = pl.pallas_call(
        functools.partial(adjoint_kernel, steps, count, blocks),
        out_shape=jax.ShapeDtypeStruct((size, cells), BF16),
        in_specs=[in_vmem] * 2 + [in_smem] + [in_vmem] * 2 + [in_smem] * 2,
        out_specs=in_vmem,
        scratch_shapes=[
            pltpu.VMEM((size, slots * block_rows), BF16),
            pltpu.VMEM((size, cells), F32),
        ],
        compiler_params=params,
        name="adjoint",
    )(total, table, rows, wide_b, held, place, step_of)

    backs = [back] + [exchange(back, "tm", d) for d in range(1, groups)]
    return pl.pallas_call(
        functools.partial(finish_kernel, groups),
        out_shape=jax.ShapeDtypeStruct(probes.shape, BF16),
        in_specs=[in_vmem] * (groups + 2),
        out_specs=in_vmem,
        compiler_params=params,
        name="finish",
    )(*backs, own, mix_b)


def solution(mesh):
    placed = (
        P(("parts", "rep"), "tm", "tile"),
        P(("parts", "tile", "tm"), None, None),
        P(("parts", "tile", "tm"), None),
        P(("parts", "tile", "tm")),
        P(("parts", "tile", "tm")),
        P(("parts", "tile", "tm")),
        P(("parts", "tile", "tm"), None),
        P(("parts", "tile", "tm")),
        P(("parts", "tile", "tm")),
        P(),
        P(),
        P(),
        P(),
    )
    return jax.shard_map(
        per_device,
        mesh=mesh,
        in_specs=placed,
        out_specs=P(("parts", "rep"), "tm", "tile"),
        check_vma=False,
    )
```

```python
import functools

import jax
import jax.numpy as jnp
from jax import lax
from jax.experimental import pallas as pl
from jax.experimental.pallas import tpu as pltpu
from jax.sharding import PartitionSpec as P

F32 = jnp.float32
BF16 = jnp.bfloat16
LANES = 128
VMEM_LIMIT = 12 * 1024 * 1024

in_vmem = pl.BlockSpec(memory_space=pltpu.VMEM)
in_hbm = pl.BlockSpec(memory_space=pltpu.HBM)
in_smem = pl.BlockSpec(memory_space=pltpu.SMEM)


def halves(value):
    high = value.astype(BF16)
    low = (value - high.astype(F32)).astype(BF16)
    return high, low


def widen(value):
    high, low = halves(value)
    return jnp.concatenate(
        [
            jnp.concatenate([high, low], axis=1),
            jnp.concatenate([high, jnp.zeros_like(low)], axis=1),
        ],
        axis=0,
    )


def times_wide(value, wide):
    high, low = halves(value)
    both = jnp.dot(
        jnp.concatenate([high, low], axis=1), wide, preferred_element_type=F32
    )
    size = both.shape[1] // 2
    return both[:, :size] + both[:, size:]


def mixing(factor, group, groups, steps, count, forward):
    block = steps * count
    row = lax.broadcasted_iota(jnp.int32, (block, groups * block), 0)
    col = lax.broadcasted_iota(jnp.int32, (block, groups * block), 1)
    peer, within = lax.div(col, block), lax.rem(col, block)
    if forward:
        row_step, row_probe = lax.div(row, count), lax.rem(row, count)
        col_probe, col_step = lax.div(within, steps), lax.rem(within, steps)
    else:
        row_probe, row_step = lax.div(row, steps), lax.rem(row, steps)
        col_step, col_probe = lax.div(within, count), lax.rem(within, count)
    value = jnp.zeros((block, groups * block), F32)
    same = row_probe == col_probe
    for other in range(groups):
        for a in range(steps):
            for b in range(steps):
                mine, theirs = group * steps + a, (group ^ other) * steps + b
                scale = factor[mine, theirs] if forward else factor[theirs, mine]
                here = same & (peer == other) & (row_step == a) & (col_step == b)
                value = jnp.where(here, scale, value)
    return jnp.concatenate(halves(value), axis=0)


def prepare_kernel(
    groups, steps, count, blocks, own_blocks,
    footprints, probes, table, temporal, row_factor, column, owner, sounding, flux_step,
    departure, counts,
    held, turned, own, table_at, rows_at, mix_f, mix_b, wide_f, wide_b, base, place, step_of,
    factor, column_at, owner_at, sounding_at, flux_at, departure_at, counts_at,
    sems, held_sems,
):
    slots = place.shape[0]
    block_rows = base.shape[1]
    pairs = [
        (temporal, factor), (column, column_at), (departure, departure_at), (owner, owner_at),
        (sounding, sounding_at), (flux_step, flux_at), (counts, counts_at), (row_factor, rows_at),
        (table, table_at), (probes, own),
    ]
    copies = [pltpu.make_async_copy(a, b, sems.at[n]) for n, (a, b) in enumerate(pairs)]
    fetches = []
    for e in range(slots):
        rows = pl.ds(e * block_rows, block_rows)
        fetches.append(
            pltpu.make_async_copy(footprints.at[rows], held.at[rows], held_sems.at[e])
        )
    for copy in copies + fetches:
        copy.start()
    for e in range(slots):
        fetches[e].wait()
        turned[:, e * block_rows : (e + 1) * block_rows] = held[
            e * block_rows : (e + 1) * block_rows, :
        ].T
    for copy in copies:
        copy.wait()
    group = lax.axis_index("tm")
    mix_f[...] = mixing(factor, group, groups, steps, count, True)
    mix_b[...] = mixing(factor, group, groups, steps, count, False)
    wide_f[...] = widen(column_at[...].T)
    wide_b[...] = widen(column_at[...])
    base[...] = jnp.zeros_like(base)
    for q in range(own_blocks):
        at = (lax.axis_index("tile") * groups + group) * own_blocks + q
        base[pl.ds(pl.multiple_of(at * count, count), count), :] = jnp.broadcast_to(
            -departure_at[q : q + 1, :], (count, block_rows)
        )
        base[pl.ds(blocks * count + at, 1), :] = jnp.full(
            (1, block_rows), counts_at[1 + q].astype(F32)
        )
        base[pl.ds(blocks * count + blocks + at, 1), :] = jnp.full(
            (1, block_rows), counts_at[1 + own_blocks + q].astype(F32)
        )
    for e in range(slots):
        place[e] = owner_at[e] * (groups * own_blocks) + sounding_at[e]
        step_of[e] = jnp.where(e < counts_at[0], flux_at[e], steps)


def row_mix(field, row_factor, transposed, wide, place, first=0):
    rows = row_factor.shape[0]
    batch = 4
    for start in range(first, first + place.shape[1] // LANES, batch):
        sums = [None] * batch
        for j in range(rows):
            tile = field[:, j * LANES : (j + 1) * LANES]
            for n in range(batch):
                i = start + n
                scale = row_factor[j, i] if transposed else row_factor[i, j]
                term = scale * tile
                sums[n] = term if sums[n] is None else sums[n] + term
        result = times_wide(jnp.concatenate(sums, axis=0), wide).astype(BF16)
        size = sums[0].shape[0]
        for n in range(batch):
            i = start + n
            place[:, (i - first) * LANES : (i - first + 1) * LANES] = result[n * size : (n + 1) * size]


def predict_kernel(groups, steps, count, *refs):
    fields = refs[:groups]
    mix_f, row_factor, wide_f, turned, base, place, step_of, total, mixed, fluxes = refs[groups:]
    block_rows = base.shape[1]
    stacked = jnp.concatenate([f[...].reshape(mixed.shape) for f in fields], axis=0)
    both = jnp.dot(mix_f[...], stacked, preferred_element_type=F32)
    size = steps * count
    mixed[...] = both[:size] + both[size:]
    row_mix(mixed, row_factor, False, wide_f[...], fluxes)
    total[...] = base[...]
    parts = jnp.dot(fluxes[...], turned[...], preferred_element_type=F32)
    for e in range(place.shape[0]):
        part = parts[:, e * block_rows : (e + 1) * block_rows]
        chosen = jnp.zeros((count, block_rows), F32)
        for t in range(steps):
            chosen = jnp.where(step_of[e] == t, part[t * count : (t + 1) * count], chosen)
        at = pl.ds(pl.multiple_of(place[e] * count, count), count)
        total[at, :] = total[at, :] + chosen


def adjoint_kernel(
    steps, count, blocks,
    total, table, row_factor, wide_b, held, place, step_of,
    back, adjoint, weights,
):
    block_rows = table.shape[1]
    slots = place.shape[0]
    lane = lax.broadcasted_iota(jnp.int32, (1, block_rows), 1).astype(F32)
    for e in range(slots):
        target = place[e]
        live = total[pl.ds(blocks * count + target, 1), :]
        error = total[pl.ds(blocks * count + blocks + target, 1), :]
        mask = jnp.where(lane < live, 1.0, 0.0)
        residual = total[pl.ds(pl.multiple_of(target * count, count), count), :] * mask
        precision = table[0]
        for n in range(1, table.shape[0]):
            precision = jnp.where(error == n, table[n], precision)
        weight = times_wide(residual, widen(precision)) * mask
        for t in range(steps):
            weights[t * count : (t + 1) * count, e * block_rows : (e + 1) * block_rows] = (
                jnp.where(step_of[e] == t, weight, 0.0).astype(BF16)
            )
    adjoint[...] = jnp.dot(weights[...], held[...], preferred_element_type=F32)
    row_mix(adjoint, row_factor, True, wide_b[...], back)


def adjoint_rest_kernel(first, adjoint, row_factor, wide_b, back):
    row_mix(adjoint, row_factor, True, wide_b[...], back, first)


def finish_kernel(groups, lanes, *refs):
    backs = refs[:groups]
    probes, mix_b, *_, out, made, sem = refs[groups:]
    stacked = jnp.concatenate([b[...] for b in backs], axis=0)
    both = jnp.dot(mix_b[...], stacked, preferred_element_type=F32)
    size = both.shape[0] // 2
    before = probes[:, :, lanes].reshape(size, both.shape[1]).astype(F32)
    after = (before + (both[:size] + both[size:])).astype(BF16)
    made[...] = after.reshape(made.shape)
    copy = pltpu.make_async_copy(made, out.at[:, :, lanes], sem)
    copy.start()
    copy.wait()


def exchange(value, axis, distance):
    size = lax.axis_size(axis)
    return lax.ppermute(value, axis, [(i, i ^ distance) for i in range(size)])


def subsets(spans):
    choices = [[]]
    for span in spans:
        choices = choices + [c + [span] for c in choices]
    return choices[1:]


def hop(value, moves):
    tiles, groups = lax.axis_size("tile"), lax.axis_size("tm")
    flip = sum(d * groups if axis == "tile" else d for axis, d in moves)
    return lax.ppermute(
        value, ("tile", "tm"), [(i, i ^ flip) for i in range(tiles * groups)]
    )


def everywhere(value):
    spans = [
        (axis, 1 << n)
        for axis in ("tm", "tile")
        for n in range(lax.axis_size(axis).bit_length() - 1)
    ]
    for start in range(0, len(spans), 2):
        sent = value.astype(BF16)
        terms = [hop(sent, moves) for moves in subsets(spans[start : start + 2])]
        for term in terms:
            value = value + term.astype(F32)
    return value


def outside(*values):
    return [pltpu.with_memory_space_constraint(x, pltpu.HBM) for x in values]


def inside(*values):
    return [pltpu.with_memory_space_constraint(x, pltpu.VMEM) for x in values]


def per_device(
    probes,
    footprints,
    owner_tile,
    sounding_index,
    flux_step,
    entry_count,
    departure,
    live_count,
    error_id,
    precision_table,
    temporal_factor,
    row_factor,
    column_factor,
):
    count, steps, cells = probes.shape
    slots, block_rows = footprints.shape[:2]
    groups = lax.axis_size("tm")
    own_blocks = departure.shape[0]
    blocks = own_blocks * groups * lax.axis_size("tile")
    size = steps * count
    params = pltpu.CompilerParams(vmem_limit_bytes=VMEM_LIMIT)

    peers = [exchange(probes, "tm", d) for d in range(1, groups)]
    held, turned, own, table, rows, mix_f, mix_b, wide_f, wide_b, base, place, step_of = (
        pl.pallas_call(
            functools.partial(prepare_kernel, groups, steps, count, blocks, own_blocks),
            out_shape=[
                pltpu.VMEM((slots * block_rows, cells), BF16),
                pltpu.VMEM((cells, slots * block_rows), BF16),
                pltpu.VMEM(probes.shape, BF16),
                pltpu.VMEM(precision_table.shape, F32),
                pltpu.SMEM(row_factor.shape, F32),
                pltpu.VMEM((2 * size, groups * size), BF16),
                pltpu.VMEM((2 * size, groups * size), BF16),
                pltpu.VMEM((2 * LANES, 2 * LANES), BF16),
                pltpu.VMEM((2 * LANES, 2 * LANES), BF16),
                pltpu.VMEM((blocks * (count + 2), block_rows), F32),
                pltpu.SMEM((slots,), jnp.int32),
                pltpu.SMEM((slots,), jnp.int32),
            ],
            in_specs=[in_hbm] * 11,
            out_specs=[in_vmem] * 4 + [in_smem] + [in_vmem] * 5 + [in_smem] * 2,
            scratch_shapes=[
                pltpu.SMEM(temporal_factor.shape, F32),
                pltpu.VMEM(column_factor.shape, F32),
                pltpu.SMEM((slots,), jnp.int32),
                pltpu.SMEM((slots,), jnp.int32),
                pltpu.SMEM((slots,), jnp.int32),
                pltpu.VMEM(departure.shape, F32),
                pltpu.SMEM((1 + 2 * own_blocks,), jnp.int32),
                pltpu.SemaphoreType.DMA((10,)),
                pltpu.SemaphoreType.DMA((slots,)),
            ],
            compiler_params=params,
            name="prepare",
        )(
            *outside(
                footprints.reshape(slots * block_rows, cells), probes, precision_table,
                temporal_factor, row_factor, column_factor, owner_tile.reshape(slots),
                sounding_index, flux_step, departure,
            ),
            jnp.concatenate([entry_count, live_count, error_id]),
        )
    )
    held, turned, own, table, mix_f, mix_b, wide_f, wide_b, base = inside(
        held, turned, own, table, mix_f, mix_b, wide_f, wide_b, base
    )

    total = pl.pallas_call(
        functools.partial(predict_kernel, groups, steps, count),
        out_shape=jax.ShapeDtypeStruct(base.shape, F32),
        in_specs=[in_vmem] * (groups + 1) + [in_smem] + [in_vmem] * 3 + [in_smem] * 2,
        out_specs=in_vmem,
        scratch_shapes=[
            pltpu.VMEM((size, cells), F32),
            pltpu.VMEM((size, cells), BF16),
        ],
        compiler_params=params,
        name="predict",
    )(own, *peers, mix_f, rows, wide_f, turned, base, place, step_of)
    total = everywhere(total)

    half = cells // 2
    low, adjoint = pl.pallas_call(
        functools.partial(adjoint_kernel, steps, count, blocks),
        out_shape=[
            jax.ShapeDtypeStruct((size, half), BF16),
            jax.ShapeDtypeStruct((size, cells), F32),
        ],
        in_specs=[in_vmem] * 2 + [in_smem] + [in_vmem] * 2 + [in_smem] * 2,
        out_specs=[in_vmem] * 2,
        scratch_shapes=[pltpu.VMEM((size, slots * block_rows), BF16)],
        compiler_params=params,
        name="adjoint",
    )(total, table, rows, wide_b, held, place, step_of)
    lows = [low] + [exchange(low, "tm", d) for d in range(1, groups)]
    high = pl.pallas_call(
        functools.partial(adjoint_rest_kernel, half // LANES),
        out_shape=jax.ShapeDtypeStruct((size, cells - half), BF16),
        in_specs=[in_vmem, in_smem, in_vmem],
        out_specs=in_vmem,
        compiler_params=params,
        name="adjoint_rest",
    )(adjoint, rows, wide_b)
    highs = [high] + [exchange(high, "tm", d) for d in range(1, groups)]

    made = []
    for lanes, backs in ((slice(0, half), lows), (slice(half, cells), highs)):
        made = [
            pl.pallas_call(
                functools.partial(finish_kernel, groups, lanes),
                out_shape=jax.ShapeDtypeStruct(probes.shape, BF16),
                in_specs=[in_vmem] * (groups + 2) + [in_hbm] * len(made),
                out_specs=in_hbm,
                input_output_aliases={groups + 2: 0} if made else {},
                scratch_shapes=[
                    pltpu.VMEM((count, steps, lanes.stop - lanes.start), BF16),
                    pltpu.SemaphoreType.DMA,
                ],
                compiler_params=params,
                name="finish",
            )(*backs, own, mix_b, *made)
        ]
    return made[0]


def solution(mesh):
    placed = (
        P(("parts", "rep"), "tm", "tile"),
        P(("parts", "tile", "tm"), None, None),
        P(("parts", "tile", "tm"), None),
        P(("parts", "tile", "tm")),
        P(("parts", "tile", "tm")),
        P(("parts", "tile", "tm")),
        P(("parts", "tile", "tm"), None),
        P(("parts", "tile", "tm")),
        P(("parts", "tile", "tm")),
        P(),
        P(),
        P(),
        P(),
    )
    return jax.shard_map(
        per_device,
        mesh=mesh,
        in_specs=placed,
        out_specs=P(("parts", "rep"), "tm", "tile"),
        check_vma=False,
    )
```

```python
import functools

import jax
import jax.numpy as jnp
from jax import lax
from jax.experimental import pallas as pl
from jax.experimental.pallas import tpu as pltpu
from jax.sharding import PartitionSpec as P

F32 = jnp.float32
BF16 = jnp.bfloat16
LANES = 128
VMEM_LIMIT = 12 * 1024 * 1024

in_vmem = pl.BlockSpec(memory_space=pltpu.VMEM)
in_hbm = pl.BlockSpec(memory_space=pltpu.HBM)
in_smem = pl.BlockSpec(memory_space=pltpu.SMEM)


def halves(value):
    high = value.astype(BF16)
    low = (value - high.astype(F32)).astype(BF16)
    return high, low


def widen(value):
    high, low = halves(value)
    return jnp.concatenate(
        [
            jnp.concatenate([high, low], axis=1),
            jnp.concatenate([high, jnp.zeros_like(low)], axis=1),
        ],
        axis=0,
    )


def times_wide(value, wide):
    high, low = halves(value)
    both = jnp.dot(
        jnp.concatenate([high, low], axis=1), wide, preferred_element_type=F32
    )
    size = both.shape[1] // 2
    return both[:, :size] + both[:, size:]


def mixing(factor, group, groups, steps, count, forward):
    block = steps * count
    row = lax.broadcasted_iota(jnp.int32, (block, groups * block), 0)
    col = lax.broadcasted_iota(jnp.int32, (block, groups * block), 1)
    peer, within = lax.div(col, block), lax.rem(col, block)
    if forward:
        row_step, row_probe = lax.div(row, count), lax.rem(row, count)
        col_probe, col_step = lax.div(within, steps), lax.rem(within, steps)
    else:
        row_probe, row_step = lax.div(row, steps), lax.rem(row, steps)
        col_step, col_probe = lax.div(within, count), lax.rem(within, count)
    value = jnp.zeros((block, groups * block), F32)
    same = row_probe == col_probe
    for other in range(groups):
        for a in range(steps):
            for b in range(steps):
                mine, theirs = group * steps + a, (group ^ other) * steps + b
                scale = factor[mine, theirs] if forward else factor[theirs, mine]
                here = same & (peer == other) & (row_step == a) & (col_step == b)
                value = jnp.where(here, scale, value)
    return jnp.concatenate(halves(value), axis=0)


def unmixing(factor, group, other, steps, count):
    block = steps * count
    row = lax.broadcasted_iota(jnp.int32, (block, block), 0)
    col = lax.broadcasted_iota(jnp.int32, (block, block), 1)
    same = lax.div(row, steps) == lax.rem(col, count)
    value = jnp.zeros((block, block), F32)
    for a in range(steps):
        for b in range(steps):
            here = same & (lax.div(col, count) == a) & (lax.rem(row, steps) == b)
            value = jnp.where(here, factor[group * steps + a, other * steps + b], value)
    high, low = halves(value)
    return jnp.concatenate(
        [
            jnp.concatenate([high, high], axis=1),
            jnp.concatenate([low, jnp.zeros_like(low)], axis=1),
        ],
        axis=0,
    )


def unmix(matrix, stacked):
    both = jnp.dot(matrix, stacked, preferred_element_type=F32)
    size = both.shape[0] // 2
    return both[:size] + both[size:]


def prepare_kernel(
    groups, steps, count, blocks, own_blocks,
    footprints, probes, table, temporal, row_factor, column, owner, sounding, flux_step,
    departure, counts,
    held, turned, own, table_at, rows_at, mix_f, mix_b, unmix_b, wide_f, wide_b, base, place, step_of,
    factor, column_at, owner_at, sounding_at, flux_at, departure_at, counts_at,
    sems, held_sems,
):
    slots = place.shape[0]
    block_rows = base.shape[1]
    pairs = [
        (temporal, factor), (column, column_at), (departure, departure_at), (owner, owner_at),
        (sounding, sounding_at), (flux_step, flux_at), (counts, counts_at), (row_factor, rows_at),
        (table, table_at), (probes, own),
    ]
    copies = [pltpu.make_async_copy(a, b, sems.at[n]) for n, (a, b) in enumerate(pairs)]
    fetches = []
    for e in range(slots):
        rows = pl.ds(e * block_rows, block_rows)
        fetches.append(
            pltpu.make_async_copy(footprints.at[rows], held.at[rows], held_sems.at[e])
        )
    for copy in copies + fetches:
        copy.start()
    for e in range(slots):
        fetches[e].wait()
        turned[:, e * block_rows : (e + 1) * block_rows] = held[
            e * block_rows : (e + 1) * block_rows, :
        ].T
    for copy in copies:
        copy.wait()
    group = lax.axis_index("tm")
    mix_f[...] = mixing(factor, group, groups, steps, count, True)
    mix_b[...] = mixing(factor, group, groups, steps, count, False)
    for other in range(groups):
        unmix_b[other] = unmixing(factor, group, group ^ other, steps, count)
    wide_f[...] = widen(column_at[...].T)
    wide_b[...] = widen(column_at[...])
    base[...] = jnp.zeros_like(base)
    for q in range(own_blocks):
        at = (lax.axis_index("tile") * groups + group) * own_blocks + q
        base[pl.ds(pl.multiple_of(at * count, count), count), :] = jnp.broadcast_to(
            -departure_at[q : q + 1, :], (count, block_rows)
        )
        base[pl.ds(blocks * count + at, 1), :] = jnp.full(
            (1, block_rows), counts_at[1 + q].astype(F32)
        )
        base[pl.ds(blocks * count + blocks + at, 1), :] = jnp.full(
            (1, block_rows), counts_at[1 + own_blocks + q].astype(F32)
        )
    for e in range(slots):
        place[e] = owner_at[e] * (groups * own_blocks) + sounding_at[e]
        step_of[e] = jnp.where(e < counts_at[0], flux_at[e], steps)


def row_mix(field, row_factor, transposed, wide, place, first=0):
    rows = row_factor.shape[0]
    batch = 4
    for start in range(first, first + place.shape[1] // LANES, batch):
        sums = [None] * batch
        for j in range(rows):
            tile = field[:, j * LANES : (j + 1) * LANES]
            for n in range(batch):
                i = start + n
                scale = row_factor[j, i] if transposed else row_factor[i, j]
                term = scale * tile
                sums[n] = term if sums[n] is None else sums[n] + term
        result = times_wide(jnp.concatenate(sums, axis=0), wide)
        size = sums[0].shape[0]
        pieces = [result.astype(BF16)] if place.shape[0] == size else halves(result)
        for n in range(batch):
            at = (start + n - first) * LANES
            for m, piece in enumerate(pieces):
                place[m * size : (m + 1) * size, at : at + LANES] = piece[n * size : (n + 1) * size]


def predict_kernel(groups, steps, count, *refs):
    fields = refs[:groups]
    (
        mix_f, row_factor, wide_f, turned, base, place, step_of,
        total, sent, mixed, fluxes,
    ) = refs[groups:]
    block_rows = base.shape[1]
    stacked = jnp.concatenate([f[...].reshape(mixed.shape) for f in fields], axis=0)
    both = jnp.dot(mix_f[...], stacked, preferred_element_type=F32)
    size = steps * count
    mixed[...] = both[:size] + both[size:]
    row_mix(mixed, row_factor, False, wide_f[...], fluxes)
    total[...] = base[...]
    parts = jnp.dot(fluxes[...], turned[...], preferred_element_type=F32)
    for e in range(place.shape[0]):
        part = parts[:, e * block_rows : (e + 1) * block_rows]
        chosen = jnp.zeros((count, block_rows), F32)
        for t in range(steps):
            chosen = jnp.where(step_of[e] == t, part[t * count : (t + 1) * count], chosen)
        at = pl.ds(pl.multiple_of(place[e] * count, count), count)
        total[at, :] = total[at, :] + chosen
    sent[...] = total[...].astype(BF16)


def adjoint_kernel(
    steps, count, blocks,
    near, far, table, row_factor, wide_b, held, place, step_of,
    back, adjoint, weights, total,
):
    total[...] = near[...] + far[...].astype(F32)
    block_rows = table.shape[1]
    slots = place.shape[0]
    lane = lax.broadcasted_iota(jnp.int32, (1, block_rows), 1).astype(F32)
    for e in range(slots):
        target = place[e]
        live = total[pl.ds(blocks * count + target, 1), :]
        error = total[pl.ds(blocks * count + blocks + target, 1), :]
        mask = jnp.where(lane < live, 1.0, 0.0)
        residual = total[pl.ds(pl.multiple_of(target * count, count), count), :] * mask
        precision = table[0]
        for n in range(1, table.shape[0]):
            precision = jnp.where(error == n, table[n], precision)
        weight = times_wide(residual, widen(precision)) * mask
        for t in range(steps):
            weights[t * count : (t + 1) * count, e * block_rows : (e + 1) * block_rows] = (
                jnp.where(step_of[e] == t, weight, 0.0).astype(BF16)
            )
    adjoint[...] = jnp.dot(weights[...], held[...], preferred_element_type=F32)
    row_mix(adjoint, row_factor, True, wide_b[...], back)


def adjoint_rest_kernel(first, adjoint, row_factor, wide_b, unmix_b, *refs):
    *sent, stacked = refs
    row_mix(adjoint, row_factor, True, wide_b[...], stacked, first)
    for n, z in enumerate(sent):
        z[...] = unmix(unmix_b[n + 1], stacked[...]).astype(BF16)


def own_kernel(lanes, probes, stacked, unmix_b, out):
    before = probes[:, :, lanes].reshape(out.shape).astype(F32)
    out[...] = before + unmix(unmix_b[0], stacked[...])


def put(value, made, out, lanes, sem):
    made[...] = value.astype(BF16).reshape(made.shape)
    copy = pltpu.make_async_copy(made, out.at[:, :, lanes], sem)
    copy.start()
    copy.wait()


def finish_low_kernel(groups, lanes, *refs):
    backs = refs[:groups]
    probes, mix_b, out, made, sem = refs[groups:]
    mixed = unmix(mix_b[...], jnp.concatenate([b[...] for b in backs], axis=0))
    put(probes[:, :, lanes].reshape(mixed.shape).astype(F32) + mixed, made, out, lanes, sem)


def finish_high_kernel(lanes, *refs):
    own, *sent, _, out, made, sem = refs
    value = own[...]
    for z in sent:
        value = value + z[...].astype(F32)
    put(value, made, out, lanes, sem)


def exchange(value, axis, distance):
    size = lax.axis_size(axis)
    return lax.ppermute(value, axis, [(i, i ^ distance) for i in range(size)])


def subsets(spans):
    choices = [[]]
    for span in spans:
        choices = choices + [c + [span] for c in choices]
    return choices[1:]


def hop(value, moves):
    tiles, groups = lax.axis_size("tile"), lax.axis_size("tm")
    flip = sum(d * groups if axis == "tile" else d for axis, d in moves)
    return lax.ppermute(
        value, ("tile", "tm"), [(i, i ^ flip) for i in range(tiles * groups)]
    )


def everywhere(value, sent):
    spans = [
        (axis, 1 << n)
        for axis in ("tm", "tile")
        for n in range(lax.axis_size(axis).bit_length() - 1)
    ]
    *terms, last = [hop(sent, moves) for moves in subsets(spans[:2])]
    for start in range(2, len(spans), 2):
        for term in terms + [last]:
            value = value + term.astype(F32)
        sent = value.astype(BF16)
        *terms, last = [hop(sent, moves) for moves in subsets(spans[start : start + 2])]
    for term in terms:
        value = value + term.astype(F32)
    return value, last


def outside(*values):
    return [pltpu.with_memory_space_constraint(x, pltpu.HBM) for x in values]


def inside(*values):
    return [pltpu.with_memory_space_constraint(x, pltpu.VMEM) for x in values]


def per_device(
    probes,
    footprints,
    owner_tile,
    sounding_index,
    flux_step,
    entry_count,
    departure,
    live_count,
    error_id,
    precision_table,
    temporal_factor,
    row_factor,
    column_factor,
):
    count, steps, cells = probes.shape
    slots, block_rows = footprints.shape[:2]
    groups = lax.axis_size("tm")
    own_blocks = departure.shape[0]
    blocks = own_blocks * groups * lax.axis_size("tile")
    size = steps * count
    params = pltpu.CompilerParams(vmem_limit_bytes=VMEM_LIMIT)

    peers = [exchange(probes, "tm", d) for d in range(1, groups)]
    held, turned, own, table, rows, mix_f, mix_b, unmix_b, wide_f, wide_b, base, place, step_of = (
        pl.pallas_call(
            functools.partial(prepare_kernel, groups, steps, count, blocks, own_blocks),
            out_shape=[
                pltpu.VMEM((slots * block_rows, cells), BF16),
                pltpu.VMEM((cells, slots * block_rows), BF16),
                pltpu.VMEM(probes.shape, BF16),
                pltpu.VMEM(precision_table.shape, F32),
                pltpu.SMEM(row_factor.shape, F32),
                pltpu.VMEM((2 * size, groups * size), BF16),
                pltpu.VMEM((2 * size, groups * size), BF16),
                pltpu.VMEM((groups, 2 * size, 2 * size), BF16),
                pltpu.VMEM((2 * LANES, 2 * LANES), BF16),
                pltpu.VMEM((2 * LANES, 2 * LANES), BF16),
                pltpu.VMEM((blocks * (count + 2), block_rows), F32),
                pltpu.SMEM((slots,), jnp.int32),
                pltpu.SMEM((slots,), jnp.int32),
            ],
            in_specs=[in_hbm] * 11,
            out_specs=[in_vmem] * 4 + [in_smem] + [in_vmem] * 6 + [in_smem] * 2,
            scratch_shapes=[
                pltpu.SMEM(temporal_factor.shape, F32),
                pltpu.VMEM(column_factor.shape, F32),
                pltpu.SMEM((slots,), jnp.int32),
                pltpu.SMEM((slots,), jnp.int32),
                pltpu.SMEM((slots,), jnp.int32),
                pltpu.VMEM(departure.shape, F32),
                pltpu.SMEM((1 + 2 * own_blocks,), jnp.int32),
                pltpu.SemaphoreType.DMA((10,)),
                pltpu.SemaphoreType.DMA((slots,)),
            ],
            compiler_params=params,
            name="prepare",
        )(
            *outside(
                footprints.reshape(slots * block_rows, cells), probes, precision_table,
                temporal_factor, row_factor, column_factor, owner_tile.reshape(slots),
                sounding_index, flux_step, departure,
            ),
            jnp.concatenate([entry_count, live_count, error_id]),
        )
    )
    held, turned, own, table, mix_f, mix_b, unmix_b, wide_f, wide_b, base = inside(
        held, turned, own, table, mix_f, mix_b, unmix_b, wide_f, wide_b, base
    )

    total, sent = pl.pallas_call(
        functools.partial(predict_kernel, groups, steps, count),
        out_shape=[
            jax.ShapeDtypeStruct(base.shape, F32),
            jax.ShapeDtypeStruct(base.shape, BF16),
        ],
        in_specs=[in_vmem] * (groups + 1) + [in_smem] + [in_vmem] * 3 + [in_smem] * 2,
        out_specs=[in_vmem] * 2,
        scratch_shapes=[
            pltpu.VMEM((size, cells), F32),
            pltpu.VMEM((size, cells), BF16),
        ],
        compiler_params=params,
        name="predict",
    )(own, *peers, mix_f, rows, wide_f, turned, base, place, step_of)
    near, far = everywhere(total, sent)

    half = cells // 2
    low, adjoint = pl.pallas_call(
        functools.partial(adjoint_kernel, steps, count, blocks),
        out_shape=[
            jax.ShapeDtypeStruct((size, half), BF16),
            jax.ShapeDtypeStruct((size, cells), F32),
        ],
        in_specs=[in_vmem] * 3 + [in_smem] + [in_vmem] * 2 + [in_smem] * 2,
        out_specs=[in_vmem] * 2,
        scratch_shapes=[
            pltpu.VMEM((size, slots * block_rows), BF16),
            pltpu.VMEM(base.shape, F32),
        ],
        compiler_params=params,
        name="adjoint",
    )(near, far, table, rows, wide_b, held, place, step_of)
    lows = [low] + [exchange(low, "tm", d) for d in range(1, groups)]
    *sent, stacked = pl.pallas_call(
        functools.partial(adjoint_rest_kernel, half // LANES),
        out_shape=[jax.ShapeDtypeStruct((size, half), BF16)] * (groups - 1)
        + [jax.ShapeDtypeStruct((2 * size, half), BF16)],
        in_specs=[in_vmem, in_smem, in_vmem, in_vmem],
        out_specs=[in_vmem] * groups,
        compiler_params=params,
        name="adjoint_rest",
    )(adjoint, rows, wide_b, unmix_b)
    highs = [exchange(z, "tm", d + 1) for d, z in enumerate(sent)]
    low_lanes, high_lanes = slice(0, half), slice(half, cells)
    high = pl.pallas_call(
        functools.partial(own_kernel, high_lanes),
        out_shape=jax.ShapeDtypeStruct((size, half), F32),
        in_specs=[in_vmem] * 3,
        out_specs=in_vmem,
        compiler_params=params,
        name="own",
    )(own, stacked, unmix_b)
    scratch = [pltpu.VMEM((count, steps, half), BF16), pltpu.SemaphoreType.DMA]
    made = pl.pallas_call(
        functools.partial(finish_low_kernel, groups, low_lanes),
        out_shape=jax.ShapeDtypeStruct(probes.shape, BF16),
        in_specs=[in_vmem] * (groups + 2),
        out_specs=in_hbm,
        scratch_shapes=scratch,
        compiler_params=params,
        name="finish_low",
    )(*lows, own, mix_b)
    return pl.pallas_call(
        functools.partial(finish_high_kernel, high_lanes),
        out_shape=jax.ShapeDtypeStruct(probes.shape, BF16),
        in_specs=[in_vmem] * groups + [in_hbm],
        out_specs=in_hbm,
        input_output_aliases={groups: 0},
        scratch_shapes=scratch,
        compiler_params=params,
        name="finish_high",
    )(high, *highs, made)


def solution(mesh):
    placed = (
        P(("parts", "rep"), "tm", "tile"),
        P(("parts", "tile", "tm"), None, None),
        P(("parts", "tile", "tm"), None),
        P(("parts", "tile", "tm")),
        P(("parts", "tile", "tm")),
        P(("parts", "tile", "tm")),
        P(("parts", "tile", "tm"), None),
        P(("parts", "tile", "tm")),
        P(("parts", "tile", "tm")),
        P(),
        P(),
        P(),
        P(),
    )
    return jax.shard_map(
        per_device,
        mesh=mesh,
        in_specs=placed,
        out_specs=P(("parts", "rep"), "tm", "tile"),
        check_vma=False,
    )
```

```python
import functools

import jax
import jax.numpy as jnp
from jax import lax
from jax.experimental import pallas as pl
from jax.experimental.pallas import tpu as pltpu
from jax.sharding import PartitionSpec as P

F32 = jnp.float32
BF16 = jnp.bfloat16
LANES = 128
VMEM_LIMIT = 12 * 1024 * 1024

in_vmem = pl.BlockSpec(memory_space=pltpu.VMEM)
in_hbm = pl.BlockSpec(memory_space=pltpu.HBM)
in_smem = pl.BlockSpec(memory_space=pltpu.SMEM)


def halves(value):
    high = value.astype(BF16)
    low = (value - high.astype(F32)).astype(BF16)
    return high, low


def widen(value):
    high, low = halves(value)
    return jnp.concatenate(
        [
            jnp.concatenate([high, low], axis=1),
            jnp.concatenate([high, jnp.zeros_like(low)], axis=1),
        ],
        axis=0,
    )


def times_wide(value, wide):
    high, low = halves(value)
    both = jnp.dot(
        jnp.concatenate([high, low], axis=1), wide, preferred_element_type=F32
    )
    size = both.shape[1] // 2
    return both[:, :size] + both[:, size:]


def mixing(factor, group, groups, steps, count, forward):
    block = steps * count
    row = lax.broadcasted_iota(jnp.int32, (block, groups * block), 0)
    col = lax.broadcasted_iota(jnp.int32, (block, groups * block), 1)
    peer, within = lax.div(col, block), lax.rem(col, block)
    if forward:
        row_step, row_probe = lax.div(row, count), lax.rem(row, count)
        col_probe, col_step = lax.div(within, steps), lax.rem(within, steps)
    else:
        row_probe, row_step = lax.div(row, steps), lax.rem(row, steps)
        col_step, col_probe = lax.div(within, count), lax.rem(within, count)
    value = jnp.zeros((block, groups * block), F32)
    same = row_probe == col_probe
    for other in range(groups):
        for a in range(steps):
            for b in range(steps):
                mine, theirs = group * steps + a, (group ^ other) * steps + b
                scale = factor[mine, theirs] if forward else factor[theirs, mine]
                here = same & (peer == other) & (row_step == a) & (col_step == b)
                value = jnp.where(here, scale, value)
    return jnp.concatenate(halves(value), axis=0)


def unmixing(factor, group, other, steps, count):
    block = steps * count
    row = lax.broadcasted_iota(jnp.int32, (block, block), 0)
    col = lax.broadcasted_iota(jnp.int32, (block, block), 1)
    same = lax.div(row, steps) == lax.rem(col, count)
    value = jnp.zeros((block, block), F32)
    for a in range(steps):
        for b in range(steps):
            here = same & (lax.div(col, count) == a) & (lax.rem(row, steps) == b)
            value = jnp.where(here, factor[group * steps + a, other * steps + b], value)
    high, low = halves(value)
    return jnp.concatenate(
        [
            jnp.concatenate([high, high], axis=1),
            jnp.concatenate([low, jnp.zeros_like(low)], axis=1),
        ],
        axis=0,
    )


def unmix(matrix, stacked):
    both = jnp.dot(matrix, stacked, preferred_element_type=F32)
    size = both.shape[0] // 2
    return both[:size] + both[size:]


def prepare_kernel(
    groups, steps, count, blocks, own_blocks,
    footprints, probes, table, temporal, row_factor, column, owner, sounding, flux_step,
    departure, counts,
    held, turned, own, table_at, rows_at, mix_f, mix_b, unmix_b, wide_f, wide_b, base, place, step_of,
    factor, column_at, owner_at, sounding_at, flux_at, departure_at, counts_at,
    sems, held_sems,
):
    slots = place.shape[0]
    block_rows = base.shape[1]
    pairs = [
        (temporal, factor), (column, column_at), (departure, departure_at), (owner, owner_at),
        (sounding, sounding_at), (flux_step, flux_at), (counts, counts_at), (row_factor, rows_at),
        (table, table_at), (probes, own),
    ]
    copies = [pltpu.make_async_copy(a, b, sems.at[n]) for n, (a, b) in enumerate(pairs)]
    fetches = []
    for e in range(slots):
        rows = pl.ds(e * block_rows, block_rows)
        fetches.append(
            pltpu.make_async_copy(footprints.at[rows], held.at[rows], held_sems.at[e])
        )
    for copy in copies + fetches:
        copy.start()
    for e in range(slots):
        fetches[e].wait()
        turned[:, e * block_rows : (e + 1) * block_rows] = held[
            e * block_rows : (e + 1) * block_rows, :
        ].T
    for copy in copies:
        copy.wait()
    group = lax.axis_index("tm")
    mix_f[...] = mixing(factor, group, groups, steps, count, True)
    mix_b[...] = mixing(factor, group, groups, steps, count, False)
    for other in range(groups):
        unmix_b[other] = unmixing(factor, group, group ^ other, steps, count)
    wide_f[...] = widen(column_at[...].T)
    wide_b[...] = widen(column_at[...])
    base[...] = jnp.zeros_like(base)
    for q in range(own_blocks):
        at = (lax.axis_index("tile") * groups + group) * own_blocks + q
        base[pl.ds(pl.multiple_of(at * count, count), count), :] = jnp.broadcast_to(
            -departure_at[q : q + 1, :], (count, block_rows)
        )
        base[pl.ds(blocks * count + at, 1), :] = jnp.full(
            (1, block_rows), counts_at[1 + q].astype(F32)
        )
        base[pl.ds(blocks * count + blocks + at, 1), :] = jnp.full(
            (1, block_rows), counts_at[1 + own_blocks + q].astype(F32)
        )
    for e in range(slots):
        place[e] = owner_at[e] * (groups * own_blocks) + sounding_at[e]
        step_of[e] = jnp.where(e < counts_at[0], flux_at[e], steps)


def row_mix(field, row_factor, transposed, wide, place, first=0):
    rows = row_factor.shape[0]
    batch = 4
    for start in range(first, first + place.shape[1] // LANES, batch):
        sums = [None] * batch
        for j in range(rows):
            tile = field[:, j * LANES : (j + 1) * LANES]
            for n in range(batch):
                i = start + n
                scale = row_factor[j, i] if transposed else row_factor[i, j]
                term = scale * tile
                sums[n] = term if sums[n] is None else sums[n] + term
        result = times_wide(jnp.concatenate(sums, axis=0), wide)
        size = sums[0].shape[0]
        pieces = [result.astype(BF16)] if place.shape[0] == size else halves(result)
        for n in range(batch):
            at = (start + n - first) * LANES
            for m, piece in enumerate(pieces):
                place[m * size : (m + 1) * size, at : at + LANES] = piece[n * size : (n + 1) * size]


def predict_kernel(groups, steps, count, *refs):
    fields = refs[:groups]
    (
        mix_f, row_factor, wide_f, turned, base, place, step_of,
        total, sent, mixed, fluxes,
    ) = refs[groups:]
    block_rows = base.shape[1]
    stacked = jnp.concatenate([f[...].reshape(mixed.shape) for f in fields], axis=0)
    both = jnp.dot(mix_f[...], stacked, preferred_element_type=F32)
    size = steps * count
    mixed[...] = both[:size] + both[size:]
    row_mix(mixed, row_factor, False, wide_f[...], fluxes)
    total[...] = base[...]
    parts = jnp.dot(fluxes[...], turned[...], preferred_element_type=F32)
    for e in range(place.shape[0]):
        part = parts[:, e * block_rows : (e + 1) * block_rows]
        chosen = jnp.zeros((count, block_rows), F32)
        for t in range(steps):
            chosen = jnp.where(step_of[e] == t, part[t * count : (t + 1) * count], chosen)
        at = pl.ds(pl.multiple_of(place[e] * count, count), count)
        total[at, :] = total[at, :] + chosen
    sent[...] = total[...].astype(BF16)


def adjoint_kernel(
    steps, count, blocks,
    near, far, table, row_factor, wide_b, held, place, step_of,
    back, adjoint, weights, total,
):
    block_rows = table.shape[1]
    slots = place.shape[0]
    lane = lax.broadcasted_iota(jnp.int32, (1, block_rows), 1).astype(F32)
    signs = slice(blocks * count, blocks * (count + 2))
    total[...] = near[signs, :] + far[signs, :].astype(F32)
    for e in range(slots):
        target = place[e]
        live = total[pl.ds(target, 1), :]
        error = total[pl.ds(blocks + target, 1), :]
        mask = jnp.where(lane < live, 1.0, 0.0)
        at = pl.ds(pl.multiple_of(target * count, count), count)
        residual = (near[at, :] + far[at, :].astype(F32)) * mask
        precision = table[0]
        for n in range(1, table.shape[0]):
            precision = jnp.where(error == n, table[n], precision)
        weight = times_wide(residual, widen(precision)) * mask
        for t in range(steps):
            weights[t * count : (t + 1) * count, e * block_rows : (e + 1) * block_rows] = (
                jnp.where(step_of[e] == t, weight, 0.0).astype(BF16)
            )
    adjoint[...] = jnp.dot(weights[...], held[...], preferred_element_type=F32)
    row_mix(adjoint, row_factor, True, wide_b[...], back)


def adjoint_rest_kernel(first, adjoint, row_factor, wide_b, unmix_b, *refs):
    *sent, stacked = refs
    row_mix(adjoint, row_factor, True, wide_b[...], stacked, first)
    for n, z in enumerate(sent):
        z[...] = unmix(unmix_b[n + 1], stacked[...]).astype(BF16)


def own_kernel(lanes, probes, stacked, unmix_b, out):
    before = probes[:, :, lanes].reshape(out.shape).astype(F32)
    out[...] = before + unmix(unmix_b[0], stacked[...])


def put(value, made, out, lanes, sem):
    made[...] = value.astype(BF16).reshape(made.shape)
    copy = pltpu.make_async_copy(made, out.at[:, :, lanes], sem)
    copy.start()
    copy.wait()


def finish_low_kernel(groups, lanes, *refs):
    backs = refs[:groups]
    probes, mix_b, out, made, sem = refs[groups:]
    mixed = unmix(mix_b[...], jnp.concatenate([b[...] for b in backs], axis=0))
    put(probes[:, :, lanes].reshape(mixed.shape).astype(F32) + mixed, made, out, lanes, sem)


def finish_high_kernel(lanes, *refs):
    own, *sent, _, out, made, sem = refs
    value = own[...]
    for z in sent:
        value = value + z[...].astype(F32)
    put(value, made, out, lanes, sem)


def exchange(value, axis, distance):
    size = lax.axis_size(axis)
    return lax.ppermute(value, axis, [(i, i ^ distance) for i in range(size)])


def subsets(spans):
    choices = [[]]
    for span in spans:
        choices = choices + [c + [span] for c in choices]
    return choices[1:]


def hop(value, moves):
    tiles, groups = lax.axis_size("tile"), lax.axis_size("tm")
    flip = sum(d * groups if axis == "tile" else d for axis, d in moves)
    return lax.ppermute(
        value, ("tile", "tm"), [(i, i ^ flip) for i in range(tiles * groups)]
    )


def everywhere(value, sent):
    spans = [
        (axis, 1 << n)
        for axis in ("tm", "tile")
        for n in range(lax.axis_size(axis).bit_length() - 1)
    ]
    *terms, last = [hop(sent, moves) for moves in subsets(spans[:2])]
    for start in range(2, len(spans), 2):
        for term in terms + [last]:
            value = value + term.astype(F32)
        sent = value.astype(BF16)
        *terms, last = [hop(sent, moves) for moves in subsets(spans[start : start + 2])]
    for term in terms:
        value = value + term.astype(F32)
    return value, last


def outside(*values):
    return [pltpu.with_memory_space_constraint(x, pltpu.HBM) for x in values]


def inside(*values):
    return [pltpu.with_memory_space_constraint(x, pltpu.VMEM) for x in values]


def per_device(
    probes,
    footprints,
    owner_tile,
    sounding_index,
    flux_step,
    entry_count,
    departure,
    live_count,
    error_id,
    precision_table,
    temporal_factor,
    row_factor,
    column_factor,
):
    count, steps, cells = probes.shape
    slots, block_rows = footprints.shape[:2]
    groups = lax.axis_size("tm")
    own_blocks = departure.shape[0]
    blocks = own_blocks * groups * lax.axis_size("tile")
    size = steps * count
    params = pltpu.CompilerParams(vmem_limit_bytes=VMEM_LIMIT)

    peers = [exchange(probes, "tm", d) for d in range(1, groups)]
    held, turned, own, table, rows, mix_f, mix_b, unmix_b, wide_f, wide_b, base, place, step_of = (
        pl.pallas_call(
            functools.partial(prepare_kernel, groups, steps, count, blocks, own_blocks),
            out_shape=[
                pltpu.VMEM((slots * block_rows, cells), BF16),
                pltpu.VMEM((cells, slots * block_rows), BF16),
                pltpu.VMEM(probes.shape, BF16),
                pltpu.VMEM(precision_table.shape, F32),
                pltpu.SMEM(row_factor.shape, F32),
                pltpu.VMEM((2 * size, groups * size), BF16),
                pltpu.VMEM((2 * size, groups * size), BF16),
                pltpu.VMEM((groups, 2 * size, 2 * size), BF16),
                pltpu.VMEM((2 * LANES, 2 * LANES), BF16),
                pltpu.VMEM((2 * LANES, 2 * LANES), BF16),
                pltpu.VMEM((blocks * (count + 2), block_rows), F32),
                pltpu.SMEM((slots,), jnp.int32),
                pltpu.SMEM((slots,), jnp.int32),
            ],
            in_specs=[in_hbm] * 11,
            out_specs=[in_vmem] * 4 + [in_smem] + [in_vmem] * 6 + [in_smem] * 2,
            scratch_shapes=[
                pltpu.SMEM(temporal_factor.shape, F32),
                pltpu.VMEM(column_factor.shape, F32),
                pltpu.SMEM((slots,), jnp.int32),
                pltpu.SMEM((slots,), jnp.int32),
                pltpu.SMEM((slots,), jnp.int32),
                pltpu.VMEM(departure.shape, F32),
                pltpu.SMEM((1 + 2 * own_blocks,), jnp.int32),
                pltpu.SemaphoreType.DMA((10,)),
                pltpu.SemaphoreType.DMA((slots,)),
            ],
            compiler_params=params,
            name="prepare",
        )(
            *outside(
                footprints.reshape(slots * block_rows, cells), probes, precision_table,
                temporal_factor, row_factor, column_factor, owner_tile.reshape(slots),
                sounding_index, flux_step, departure,
            ),
            jnp.concatenate([entry_count, live_count, error_id]),
        )
    )
    held, turned, own, table, mix_f, mix_b, unmix_b, wide_f, wide_b, base = inside(
        held, turned, own, table, mix_f, mix_b, unmix_b, wide_f, wide_b, base
    )

    total, sent = pl.pallas_call(
        functools.partial(predict_kernel, groups, steps, count),
        out_shape=[
            jax.ShapeDtypeStruct(base.shape, F32),
            jax.ShapeDtypeStruct(base.shape, BF16),
        ],
        in_specs=[in_vmem] * (groups + 1) + [in_smem] + [in_vmem] * 3 + [in_smem] * 2,
        out_specs=[in_vmem] * 2,
        scratch_shapes=[
            pltpu.VMEM((size, cells), F32),
            pltpu.VMEM((size, cells), BF16),
        ],
        compiler_params=params,
        name="predict",
    )(own, *peers, mix_f, rows, wide_f, turned, base, place, step_of)
    near, far = everywhere(total, sent)

    half = cells // 2
    low, adjoint = pl.pallas_call(
        functools.partial(adjoint_kernel, steps, count, blocks),
        out_shape=[
            jax.ShapeDtypeStruct((size, half), BF16),
            jax.ShapeDtypeStruct((size, cells), F32),
        ],
        in_specs=[in_vmem] * 3 + [in_smem] + [in_vmem] * 2 + [in_smem] * 2,
        out_specs=[in_vmem] * 2,
        scratch_shapes=[
            pltpu.VMEM((size, slots * block_rows), BF16),
            pltpu.VMEM((2 * blocks, block_rows), F32),
        ],
        compiler_params=params,
        name="adjoint",
    )(near, far, table, rows, wide_b, held, place, step_of)
    lows = [low] + [exchange(low, "tm", d) for d in range(1, groups)]
    *sent, stacked = pl.pallas_call(
        functools.partial(adjoint_rest_kernel, half // LANES),
        out_shape=[jax.ShapeDtypeStruct((size, half), BF16)] * (groups - 1)
        + [jax.ShapeDtypeStruct((2 * size, half), BF16)],
        in_specs=[in_vmem, in_smem, in_vmem, in_vmem],
        out_specs=[in_vmem] * groups,
        compiler_params=params,
        name="adjoint_rest",
    )(adjoint, rows, wide_b, unmix_b)
    highs = [exchange(z, "tm", d + 1) for d, z in enumerate(sent)]
    low_lanes, high_lanes = slice(0, half), slice(half, cells)
    high = pl.pallas_call(
        functools.partial(own_kernel, high_lanes),
        out_shape=jax.ShapeDtypeStruct((size, half), F32),
        in_specs=[in_vmem] * 3,
        out_specs=in_vmem,
        compiler_params=params,
        name="own",
    )(own, stacked, unmix_b)
    scratch = [pltpu.VMEM((count, steps, half), BF16), pltpu.SemaphoreType.DMA]
    made = pl.pallas_call(
        functools.partial(finish_low_kernel, groups, low_lanes),
        out_shape=jax.ShapeDtypeStruct(probes.shape, BF16),
        in_specs=[in_vmem] * (groups + 2),
        out_specs=in_hbm,
        scratch_shapes=scratch,
        compiler_params=params,
        name="finish_low",
    )(*lows, own, mix_b)
    return pl.pallas_call(
        functools.partial(finish_high_kernel, high_lanes),
        out_shape=jax.ShapeDtypeStruct(probes.shape, BF16),
        in_specs=[in_vmem] * groups + [in_hbm],
        out_specs=in_hbm,
        input_output_aliases={groups: 0},
        scratch_shapes=scratch,
        compiler_params=params,
        name="finish_high",
    )(high, *highs, made)


def solution(mesh):
    placed = (
        P(("parts", "rep"), "tm", "tile"),
        P(("parts", "tile", "tm"), None, None),
        P(("parts", "tile", "tm"), None),
        P(("parts", "tile", "tm")),
        P(("parts", "tile", "tm")),
        P(("parts", "tile", "tm")),
        P(("parts", "tile", "tm"), None),
        P(("parts", "tile", "tm")),
        P(("parts", "tile", "tm")),
        P(),
        P(),
        P(),
        P(),
    )
    return jax.shard_map(
        per_device,
        mesh=mesh,
        in_specs=placed,
        out_specs=P(("parts", "rep"), "tm", "tile"),
        check_vma=False,
    )
```

```python
import functools

import jax
import jax.numpy as jnp
from jax import lax
from jax.experimental import pallas as pl
from jax.experimental.pallas import tpu as pltpu
from jax.sharding import PartitionSpec as P

F32 = jnp.float32
BF16 = jnp.bfloat16
LANES = 128
VMEM_LIMIT = 12 * 1024 * 1024

in_vmem = pl.BlockSpec(memory_space=pltpu.VMEM)
in_hbm = pl.BlockSpec(memory_space=pltpu.HBM)
in_smem = pl.BlockSpec(memory_space=pltpu.SMEM)


def halves(value):
    high = value.astype(BF16)
    low = (value - high.astype(F32)).astype(BF16)
    return high, low


def widen(value):
    high, low = halves(value)
    return jnp.concatenate(
        [
            jnp.concatenate([high, low], axis=1),
            jnp.concatenate([high, jnp.zeros_like(low)], axis=1),
        ],
        axis=0,
    )


def times_wide(value, wide):
    high, low = halves(value)
    both = jnp.dot(
        jnp.concatenate([high, low], axis=1), wide, preferred_element_type=F32
    )
    size = both.shape[1] // 2
    return both[:, :size] + both[:, size:]


def mixing(factor, group, groups, steps, count, forward):
    block = steps * count
    row = lax.broadcasted_iota(jnp.int32, (block, groups * block), 0)
    col = lax.broadcasted_iota(jnp.int32, (block, groups * block), 1)
    peer, within = lax.div(col, block), lax.rem(col, block)
    if forward:
        row_step, row_probe = lax.div(row, count), lax.rem(row, count)
        col_probe, col_step = lax.div(within, steps), lax.rem(within, steps)
    else:
        row_probe, row_step = lax.div(row, steps), lax.rem(row, steps)
        col_step, col_probe = lax.div(within, count), lax.rem(within, count)
    value = jnp.zeros((block, groups * block), F32)
    same = row_probe == col_probe
    for other in range(groups):
        for a in range(steps):
            for b in range(steps):
                mine, theirs = group * steps + a, (group ^ other) * steps + b
                scale = factor[mine, theirs] if forward else factor[theirs, mine]
                here = same & (peer == other) & (row_step == a) & (col_step == b)
                value = jnp.where(here, scale, value)
    return jnp.concatenate(halves(value), axis=0)


def unmixing(factor, group, other, steps, count):
    block = steps * count
    row = lax.broadcasted_iota(jnp.int32, (block, block), 0)
    col = lax.broadcasted_iota(jnp.int32, (block, block), 1)
    same = lax.div(row, steps) == lax.rem(col, count)
    value = jnp.zeros((block, block), F32)
    for a in range(steps):
        for b in range(steps):
            here = same & (lax.div(col, count) == a) & (lax.rem(row, steps) == b)
            value = jnp.where(here, factor[group * steps + a, other * steps + b], value)
    high, low = halves(value)
    return jnp.concatenate(
        [
            jnp.concatenate([high, high], axis=1),
            jnp.concatenate([low, jnp.zeros_like(low)], axis=1),
        ],
        axis=0,
    )


def unmix(matrix, stacked):
    both = jnp.dot(matrix, stacked, preferred_element_type=F32)
    size = both.shape[0] // 2
    return both[:size] + both[size:]


def prepare_kernel(
    groups, steps, count, blocks, own_blocks,
    footprints, probes, table, temporal, row_factor, column, owner, sounding, flux_step,
    departure, counts,
    held, turned, own, table_at, rows_at, mix_f, mix_b, unmix_b, wide_f, wide_b, base, place, step_of,
    factor, column_at, owner_at, sounding_at, flux_at, departure_at, counts_at,
    sems, held_sems,
):
    slots = place.shape[0]
    block_rows = base.shape[1]
    pairs = [
        (temporal, factor), (column, column_at), (departure, departure_at), (owner, owner_at),
        (sounding, sounding_at), (flux_step, flux_at), (counts, counts_at), (row_factor, rows_at),
        (table, table_at), (probes, own),
    ]
    copies = [pltpu.make_async_copy(a, b, sems.at[n]) for n, (a, b) in enumerate(pairs)]
    fetches = []
    for e in range(slots):
        rows = pl.ds(e * block_rows, block_rows)
        fetches.append(
            pltpu.make_async_copy(footprints.at[rows], held.at[rows], held_sems.at[e])
        )
    for copy in copies + fetches:
        copy.start()
    for e in range(slots):
        fetches[e].wait()
        turned[:, e * block_rows : (e + 1) * block_rows] = held[
            e * block_rows : (e + 1) * block_rows, :
        ].T
    for copy in copies:
        copy.wait()
    group = lax.axis_index("tm")
    mix_f[...] = mixing(factor, group, groups, steps, count, True)
    mix_b[...] = mixing(factor, group, groups, steps, count, False)
    for other in range(groups):
        unmix_b[other] = unmixing(factor, group, group ^ other, steps, count)
    wide_f[...] = widen(column_at[...].T)
    wide_b[...] = widen(column_at[...])
    base[...] = jnp.zeros_like(base)
    for q in range(own_blocks):
        at = (lax.axis_index("tile") * groups + group) * own_blocks + q
        base[pl.ds(pl.multiple_of(at * count, count), count), :] = jnp.broadcast_to(
            -departure_at[q : q + 1, :], (count, block_rows)
        )
        base[pl.ds(blocks * count + at, 1), :] = jnp.full(
            (1, block_rows), counts_at[1 + q].astype(F32)
        )
        base[pl.ds(blocks * count + blocks + at, 1), :] = jnp.full(
            (1, block_rows), counts_at[1 + own_blocks + q].astype(F32)
        )
    for e in range(slots):
        place[e] = owner_at[e] * (groups * own_blocks) + sounding_at[e]
        step_of[e] = jnp.where(e < counts_at[0], flux_at[e], steps)


def row_mix(field, row_factor, transposed, wide, place, first=0):
    rows = row_factor.shape[0]
    batch = 4
    for start in range(first, first + place.shape[1] // LANES, batch):
        sums = [None] * batch
        for j in range(rows):
            tile = field[:, j * LANES : (j + 1) * LANES]
            for n in range(batch):
                i = start + n
                scale = row_factor[j, i] if transposed else row_factor[i, j]
                term = scale * tile
                sums[n] = term if sums[n] is None else sums[n] + term
        result = times_wide(jnp.concatenate(sums, axis=0), wide)
        size = sums[0].shape[0]
        pieces = [result.astype(BF16)] if place.shape[0] == size else halves(result)
        for n in range(batch):
            at = (start + n - first) * LANES
            for m, piece in enumerate(pieces):
                place[m * size : (m + 1) * size, at : at + LANES] = piece[n * size : (n + 1) * size]


def predict_kernel(groups, steps, count, *refs):
    fields = refs[:groups]
    (
        mix_f, row_factor, wide_f, turned, base, place, step_of,
        total, sent, mixed, fluxes,
    ) = refs[groups:]
    block_rows = base.shape[1]
    stacked = jnp.concatenate([f[...].reshape(mixed.shape) for f in fields], axis=0)
    both = jnp.dot(mix_f[...], stacked, preferred_element_type=F32)
    size = steps * count
    mixed[...] = both[:size] + both[size:]
    row_mix(mixed, row_factor, False, wide_f[...], fluxes)
    total[...] = base[...]
    parts = jnp.dot(fluxes[...], turned[...], preferred_element_type=F32)
    for e in range(place.shape[0]):
        part = parts[:, e * block_rows : (e + 1) * block_rows]
        chosen = jnp.zeros((count, block_rows), F32)
        for t in range(steps):
            chosen = jnp.where(step_of[e] == t, part[t * count : (t + 1) * count], chosen)
        at = pl.ds(pl.multiple_of(place[e] * count, count), count)
        total[at, :] = total[at, :] + chosen
    sent[...] = total[...].astype(BF16)


def adjoint_kernel(
    steps, count, blocks,
    near, far, table, row_factor, wide_b, held, place, step_of,
    back, adjoint, weights, total,
):
    total[...] = near[...] + far[...].astype(F32)
    block_rows = table.shape[1]
    slots = place.shape[0]
    lane = lax.broadcasted_iota(jnp.int32, (1, block_rows), 1).astype(F32)
    for e in range(slots):
        target = place[e]
        live = total[pl.ds(blocks * count + target, 1), :]
        error = total[pl.ds(blocks * count + blocks + target, 1), :]
        mask = jnp.where(lane < live, 1.0, 0.0)
        residual = total[pl.ds(pl.multiple_of(target * count, count), count), :] * mask
        precision = table[0]
        for n in range(1, table.shape[0]):
            precision = jnp.where(error == n, table[n], precision)
        weight = times_wide(residual, widen(precision)) * mask
        for t in range(steps):
            weights[t * count : (t + 1) * count, e * block_rows : (e + 1) * block_rows] = (
                jnp.where(step_of[e] == t, weight, 0.0).astype(BF16)
            )
    adjoint[...] = jnp.dot(weights[...], held[...], preferred_element_type=F32)
    row_mix(adjoint, row_factor, True, wide_b[...], back)


def adjoint_rest_kernel(first, adjoint, row_factor, wide_b, unmix_b, *refs):
    *sent, stacked = refs
    row_mix(adjoint, row_factor, True, wide_b[...], stacked, first)
    for n, z in enumerate(sent):
        z[...] = unmix(unmix_b[n + 1][:, : stacked.shape[0]], stacked[...]).astype(BF16)


def own_kernel(lanes, probes, stacked, unmix_b, out):
    before = probes[:, :, lanes].reshape(out.shape).astype(F32)
    out[...] = before + unmix(unmix_b[0][:, : stacked.shape[0]], stacked[...])


def put(value, made, out, lanes, sem):
    made[...] = value.astype(BF16).reshape(made.shape)
    copy = pltpu.make_async_copy(made, out.at[:, :, lanes], sem)
    copy.start()
    copy.wait()


def finish_low_kernel(groups, lanes, *refs):
    backs = refs[:groups]
    probes, mix_b, out, made, sem = refs[groups:]
    mixed = unmix(mix_b[...], jnp.concatenate([b[...] for b in backs], axis=0))
    put(probes[:, :, lanes].reshape(mixed.shape).astype(F32) + mixed, made, out, lanes, sem)


def finish_high_kernel(lanes, *refs):
    own, *sent, _, out, made, sem = refs
    value = own[...]
    for z in sent:
        value = value + z[...].astype(F32)
    put(value, made, out, lanes, sem)


def exchange(value, axis, distance):
    size = lax.axis_size(axis)
    return lax.ppermute(value, axis, [(i, i ^ distance) for i in range(size)])


def subsets(spans):
    choices = [[]]
    for span in spans:
        choices = choices + [c + [span] for c in choices]
    return choices[1:]


def hop(value, moves):
    tiles, groups = lax.axis_size("tile"), lax.axis_size("tm")
    flip = sum(d * groups if axis == "tile" else d for axis, d in moves)
    return lax.ppermute(
        value, ("tile", "tm"), [(i, i ^ flip) for i in range(tiles * groups)]
    )


def everywhere(value, sent):
    spans = [
        (axis, 1 << n)
        for axis in ("tm", "tile")
        for n in range(lax.axis_size(axis).bit_length() - 1)
    ]
    *terms, last = [hop(sent, moves) for moves in subsets(spans[:2])]
    for start in range(2, len(spans), 2):
        for term in terms + [last]:
            value = value + term.astype(F32)
        sent = value.astype(BF16)
        *terms, last = [hop(sent, moves) for moves in subsets(spans[start : start + 2])]
    for term in terms:
        value = value + term.astype(F32)
    return value, last


def outside(*values):
    return [pltpu.with_memory_space_constraint(x, pltpu.HBM) for x in values]


def inside(*values):
    return [pltpu.with_memory_space_constraint(x, pltpu.VMEM) for x in values]


def per_device(
    probes,
    footprints,
    owner_tile,
    sounding_index,
    flux_step,
    entry_count,
    departure,
    live_count,
    error_id,
    precision_table,
    temporal_factor,
    row_factor,
    column_factor,
):
    count, steps, cells = probes.shape
    slots, block_rows = footprints.shape[:2]
    groups = lax.axis_size("tm")
    own_blocks = departure.shape[0]
    blocks = own_blocks * groups * lax.axis_size("tile")
    size = steps * count
    params = pltpu.CompilerParams(vmem_limit_bytes=VMEM_LIMIT)

    peers = [exchange(probes, "tm", d) for d in range(1, groups)]
    held, turned, own, table, rows, mix_f, mix_b, unmix_b, wide_f, wide_b, base, place, step_of = (
        pl.pallas_call(
            functools.partial(prepare_kernel, groups, steps, count, blocks, own_blocks),
            out_shape=[
                pltpu.VMEM((slots * block_rows, cells), BF16),
                pltpu.VMEM((cells, slots * block_rows), BF16),
                pltpu.VMEM(probes.shape, BF16),
                pltpu.VMEM(precision_table.shape, F32),
                pltpu.SMEM(row_factor.shape, F32),
                pltpu.VMEM((2 * size, groups * size), BF16),
                pltpu.VMEM((2 * size, groups * size), BF16),
                pltpu.VMEM((groups, 2 * size, 2 * size), BF16),
                pltpu.VMEM((2 * LANES, 2 * LANES), BF16),
                pltpu.VMEM((2 * LANES, 2 * LANES), BF16),
                pltpu.VMEM((blocks * (count + 2), block_rows), F32),
                pltpu.SMEM((slots,), jnp.int32),
                pltpu.SMEM((slots,), jnp.int32),
            ],
            in_specs=[in_hbm] * 11,
            out_specs=[in_vmem] * 4 + [in_smem] + [in_vmem] * 6 + [in_smem] * 2,
            scratch_shapes=[
                pltpu.SMEM(temporal_factor.shape, F32),
                pltpu.VMEM(column_factor.shape, F32),
                pltpu.SMEM((slots,), jnp.int32),
                pltpu.SMEM((slots,), jnp.int32),
                pltpu.SMEM((slots,), jnp.int32),
                pltpu.VMEM(departure.shape, F32),
                pltpu.SMEM((1 + 2 * own_blocks,), jnp.int32),
                pltpu.SemaphoreType.DMA((10,)),
                pltpu.SemaphoreType.DMA((slots,)),
            ],
            compiler_params=params,
            name="prepare",
        )(
            *outside(
                footprints.reshape(slots * block_rows, cells), probes, precision_table,
                temporal_factor, row_factor, column_factor, owner_tile.reshape(slots),
                sounding_index, flux_step, departure,
            ),
            jnp.concatenate([entry_count, live_count, error_id]),
        )
    )
    held, turned, own, table, mix_f, mix_b, unmix_b, wide_f, wide_b, base = inside(
        held, turned, own, table, mix_f, mix_b, unmix_b, wide_f, wide_b, base
    )

    total, sent = pl.pallas_call(
        functools.partial(predict_kernel, groups, steps, count),
        out_shape=[
            jax.ShapeDtypeStruct(base.shape, F32),
            jax.ShapeDtypeStruct(base.shape, BF16),
        ],
        in_specs=[in_vmem] * (groups + 1) + [in_smem] + [in_vmem] * 3 + [in_smem] * 2,
        out_specs=[in_vmem] * 2,
        scratch_shapes=[
            pltpu.VMEM((size, cells), F32),
            pltpu.VMEM((size, cells), BF16),
        ],
        compiler_params=params,
        name="predict",
    )(own, *peers, mix_f, rows, wide_f, turned, base, place, step_of)
    near, far = everywhere(total, sent)

    half = cells // 2
    low, adjoint = pl.pallas_call(
        functools.partial(adjoint_kernel, steps, count, blocks),
        out_shape=[
            jax.ShapeDtypeStruct((size, half), BF16),
            jax.ShapeDtypeStruct((size, cells), F32),
        ],
        in_specs=[in_vmem] * 3 + [in_smem] + [in_vmem] * 2 + [in_smem] * 2,
        out_specs=[in_vmem] * 2,
        scratch_shapes=[
            pltpu.VMEM((size, slots * block_rows), BF16),
            pltpu.VMEM(base.shape, F32),
        ],
        compiler_params=params,
        name="adjoint",
    )(near, far, table, rows, wide_b, held, place, step_of)
    lows = [low] + [exchange(low, "tm", d) for d in range(1, groups)]
    *sent, stacked = pl.pallas_call(
        functools.partial(adjoint_rest_kernel, half // LANES),
        out_shape=[jax.ShapeDtypeStruct((size, half), BF16)] * (groups - 1)
        + [jax.ShapeDtypeStruct((size, half), BF16)],
        in_specs=[in_vmem, in_smem, in_vmem, in_vmem],
        out_specs=[in_vmem] * groups,
        compiler_params=params,
        name="adjoint_rest",
    )(adjoint, rows, wide_b, unmix_b)
    highs = [exchange(z, "tm", d + 1) for d, z in enumerate(sent)]
    low_lanes, high_lanes = slice(0, half), slice(half, cells)
    high = pl.pallas_call(
        functools.partial(own_kernel, high_lanes),
        out_shape=jax.ShapeDtypeStruct((size, half), F32),
        in_specs=[in_vmem] * 3,
        out_specs=in_vmem,
        compiler_params=params,
        name="own",
    )(own, stacked, unmix_b)
    scratch = [pltpu.VMEM((count, steps, half), BF16), pltpu.SemaphoreType.DMA]
    made = pl.pallas_call(
        functools.partial(finish_low_kernel, groups, low_lanes),
        out_shape=jax.ShapeDtypeStruct(probes.shape, BF16),
        in_specs=[in_vmem] * (groups + 2),
        out_specs=in_hbm,
        scratch_shapes=scratch,
        compiler_params=params,
        name="finish_low",
    )(*lows, own, mix_b)
    return pl.pallas_call(
        functools.partial(finish_high_kernel, high_lanes),
        out_shape=jax.ShapeDtypeStruct(probes.shape, BF16),
        in_specs=[in_vmem] * groups + [in_hbm],
        out_specs=in_hbm,
        input_output_aliases={groups: 0},
        scratch_shapes=scratch,
        compiler_params=params,
        name="finish_high",
    )(high, *highs, made)


def solution(mesh):
    placed = (
        P(("parts", "rep"), "tm", "tile"),
        P(("parts", "tile", "tm"), None, None),
        P(("parts", "tile", "tm"), None),
        P(("parts", "tile", "tm")),
        P(("parts", "tile", "tm")),
        P(("parts", "tile", "tm")),
        P(("parts", "tile", "tm"), None),
        P(("parts", "tile", "tm")),
        P(("parts", "tile", "tm")),
        P(),
        P(),
        P(),
        P(),
    )
    return jax.shard_map(
        per_device,
        mesh=mesh,
        in_specs=placed,
        out_specs=P(("parts", "rep"), "tm", "tile"),
        check_vma=False,
    )
```

```python
import functools

import jax
import jax.numpy as jnp
from jax import lax
from jax.experimental import pallas as pl
from jax.experimental.pallas import tpu as pltpu
from jax.sharding import PartitionSpec as P

F32 = jnp.float32
BF16 = jnp.bfloat16
LANES = 128
VMEM_LIMIT = 12 * 1024 * 1024

in_vmem = pl.BlockSpec(memory_space=pltpu.VMEM)
in_hbm = pl.BlockSpec(memory_space=pltpu.HBM)
in_smem = pl.BlockSpec(memory_space=pltpu.SMEM)


def halves(value):
    high = value.astype(BF16)
    low = (value - high.astype(F32)).astype(BF16)
    return high, low


def widen(value):
    high, low = halves(value)
    return jnp.concatenate(
        [
            jnp.concatenate([high, low], axis=1),
            jnp.concatenate([high, jnp.zeros_like(low)], axis=1),
        ],
        axis=0,
    )


def times_wide(value, wide):
    high, low = halves(value)
    both = jnp.dot(
        jnp.concatenate([high, low], axis=1), wide, preferred_element_type=F32
    )
    size = both.shape[1] // 2
    return both[:, :size] + both[:, size:]


def mixing(factor, group, groups, steps, count, forward):
    block = steps * count
    row = lax.broadcasted_iota(jnp.int32, (block, groups * block), 0)
    col = lax.broadcasted_iota(jnp.int32, (block, groups * block), 1)
    peer, within = lax.div(col, block), lax.rem(col, block)
    if forward:
        row_step, row_probe = lax.div(row, count), lax.rem(row, count)
        col_probe, col_step = lax.div(within, steps), lax.rem(within, steps)
    else:
        row_probe, row_step = lax.div(row, steps), lax.rem(row, steps)
        col_step, col_probe = lax.div(within, count), lax.rem(within, count)
    value = jnp.zeros((block, groups * block), F32)
    same = row_probe == col_probe
    for other in range(groups):
        for a in range(steps):
            for b in range(steps):
                mine, theirs = group * steps + a, (group ^ other) * steps + b
                scale = factor[mine, theirs] if forward else factor[theirs, mine]
                here = same & (peer == other) & (row_step == a) & (col_step == b)
                value = jnp.where(here, scale, value)
    return jnp.concatenate(halves(value), axis=0)


def unmixing(factor, group, other, steps, count):
    block = steps * count
    row = lax.broadcasted_iota(jnp.int32, (block, block), 0)
    col = lax.broadcasted_iota(jnp.int32, (block, block), 1)
    same = lax.div(row, steps) == lax.rem(col, count)
    value = jnp.zeros((block, block), F32)
    for a in range(steps):
        for b in range(steps):
            here = same & (lax.div(col, count) == a) & (lax.rem(row, steps) == b)
            value = jnp.where(here, factor[group * steps + a, other * steps + b], value)
    high, low = halves(value)
    return jnp.concatenate(
        [
            jnp.concatenate([high, high], axis=1),
            jnp.concatenate([low, jnp.zeros_like(low)], axis=1),
        ],
        axis=0,
    )


def unmix(matrix, stacked):
    both = jnp.dot(matrix, stacked, preferred_element_type=F32)
    size = both.shape[0] // 2
    return both[:size] + both[size:]


def prepare_kernel(
    groups, steps, count, blocks, own_blocks,
    footprints, probes, table, temporal, row_factor, column, owner, sounding, flux_step,
    departure, counts,
    held, turned, own, table_at, rows_at, mix_f, mix_b, unmix_b, wide_f, wide_b, base, place, step_of,
    factor, column_at, owner_at, sounding_at, flux_at, departure_at, counts_at,
    sems, held_sems,
):
    slots = place.shape[0]
    block_rows = base.shape[1]
    pairs = [
        (temporal, factor), (column, column_at), (departure, departure_at), (owner, owner_at),
        (sounding, sounding_at), (flux_step, flux_at), (counts, counts_at), (row_factor, rows_at),
        (table, table_at), (probes, own),
    ]
    copies = [pltpu.make_async_copy(a, b, sems.at[n]) for n, (a, b) in enumerate(pairs)]
    fetches = []
    for e in range(slots):
        rows = pl.ds(e * block_rows, block_rows)
        fetches.append(
            pltpu.make_async_copy(footprints.at[rows], held.at[rows], held_sems.at[e])
        )
    for copy in copies + fetches:
        copy.start()
    for e in range(slots):
        fetches[e].wait()
        turned[:, e * block_rows : (e + 1) * block_rows] = held[
            e * block_rows : (e + 1) * block_rows, :
        ].T
    for copy in copies:
        copy.wait()
    group = lax.axis_index("tm")
    mix_f[...] = mixing(factor, group, groups, steps, count, True)
    mix_b[...] = mixing(factor, group, groups, steps, count, False)
    for other in range(groups):
        unmix_b[other] = unmixing(factor, group, group ^ other, steps, count)
    wide_f[...] = widen(column_at[...].T)
    wide_b[...] = widen(column_at[...])
    base[...] = jnp.zeros_like(base)
    for q in range(own_blocks):
        at = (lax.axis_index("tile") * groups + group) * own_blocks + q
        base[pl.ds(pl.multiple_of(at * count, count), count), :] = jnp.broadcast_to(
            -departure_at[q : q + 1, :], (count, block_rows)
        )
        base[pl.ds(blocks * count + at, 1), :] = jnp.full(
            (1, block_rows), counts_at[1 + q].astype(F32)
        )
        base[pl.ds(blocks * count + blocks + at, 1), :] = jnp.full(
            (1, block_rows), counts_at[1 + own_blocks + q].astype(F32)
        )
    for e in range(slots):
        place[e] = owner_at[e] * (groups * own_blocks) + sounding_at[e]
        step_of[e] = jnp.where(e < counts_at[0], flux_at[e], steps)


def row_mix(field, row_factor, transposed, wide, place, first=0):
    rows = row_factor.shape[0]
    batch = 4
    for start in range(first, first + place.shape[1] // LANES, batch):
        sums = [None] * batch
        for j in range(rows):
            tile = field[:, j * LANES : (j + 1) * LANES]
            for n in range(batch):
                i = start + n
                scale = row_factor[j, i] if transposed else row_factor[i, j]
                term = scale * tile
                sums[n] = term if sums[n] is None else sums[n] + term
        result = times_wide(jnp.concatenate(sums, axis=0), wide)
        size = sums[0].shape[0]
        pieces = [result.astype(BF16)] if place.shape[0] == size else halves(result)
        for n in range(batch):
            at = (start + n - first) * LANES
            for m, piece in enumerate(pieces):
                place[m * size : (m + 1) * size, at : at + LANES] = piece[n * size : (n + 1) * size]


def predict_kernel(groups, steps, count, *refs):
    fields = refs[:groups]
    (
        mix_f, row_factor, wide_f, turned, base, place, step_of,
        total, sent, mixed, fluxes,
    ) = refs[groups:]
    block_rows = base.shape[1]
    stacked = jnp.concatenate([f[...].reshape(mixed.shape) for f in fields], axis=0)
    both = jnp.dot(mix_f[...], stacked, preferred_element_type=F32)
    size = steps * count
    mixed[...] = both[:size] + both[size:]
    row_mix(mixed, row_factor, False, wide_f[...], fluxes)
    total[...] = base[...]
    parts = jnp.dot(fluxes[...], turned[...], preferred_element_type=F32)
    for e in range(place.shape[0]):
        part = parts[:, e * block_rows : (e + 1) * block_rows]
        chosen = jnp.zeros((count, block_rows), F32)
        for t in range(steps):
            chosen = jnp.where(step_of[e] == t, part[t * count : (t + 1) * count], chosen)
        at = pl.ds(pl.multiple_of(place[e] * count, count), count)
        total[at, :] = total[at, :] + chosen
    sent[...] = total[...].astype(BF16)


def adjoint_kernel(
    steps, count, blocks,
    near, far, table, row_factor, wide_b, held, place, step_of,
    back, adjoint, weights, total,
):
    block_rows = table.shape[1]
    slots = place.shape[0]
    lane = lax.broadcasted_iota(jnp.int32, (1, block_rows), 1).astype(F32)
    signs = slice(blocks * count, blocks * (count + 2))
    total[...] = near[signs, :] + far[signs, :].astype(F32)
    for e in range(slots):
        target = place[e]
        live = total[pl.ds(target, 1), :]
        error = total[pl.ds(blocks + target, 1), :]
        mask = jnp.where(lane < live, 1.0, 0.0)
        at = pl.ds(pl.multiple_of(target * count, count), count)
        residual = (near[at, :] + far[at, :].astype(F32)) * mask
        precision = table[0]
        for n in range(1, table.shape[0]):
            precision = jnp.where(error == n, table[n], precision)
        weight = times_wide(residual, widen(precision)) * mask
        for t in range(steps):
            weights[t * count : (t + 1) * count, e * block_rows : (e + 1) * block_rows] = (
                jnp.where(step_of[e] == t, weight, 0.0).astype(BF16)
            )
    adjoint[...] = jnp.dot(weights[...], held[...], preferred_element_type=F32)
    row_mix(adjoint, row_factor, True, wide_b[...], back)


def adjoint_rest_kernel(first, adjoint, row_factor, wide_b, unmix_b, *refs):
    *sent, stacked = refs
    row_mix(adjoint, row_factor, True, wide_b[...], stacked, first)
    for n, z in enumerate(sent):
        z[...] = unmix(unmix_b[n + 1][:, : stacked.shape[0]], stacked[...]).astype(BF16)


def own_kernel(lanes, probes, stacked, unmix_b, out):
    before = probes[:, :, lanes].reshape(out.shape).astype(F32)
    out[...] = before + unmix(unmix_b[0][:, : stacked.shape[0]], stacked[...])


def put(value, made, out, lanes, sem):
    made[...] = value.astype(BF16).reshape(made.shape)
    copy = pltpu.make_async_copy(made, out.at[:, :, lanes], sem)
    copy.start()
    copy.wait()


def finish_low_kernel(groups, lanes, *refs):
    backs = refs[:groups]
    probes, mix_b, out, made, sem = refs[groups:]
    mixed = unmix(mix_b[...], jnp.concatenate([b[...] for b in backs], axis=0))
    put(probes[:, :, lanes].reshape(mixed.shape).astype(F32) + mixed, made, out, lanes, sem)


def finish_high_kernel(lanes, *refs):
    own, *sent, _, out, made, sem = refs
    value = own[...]
    for z in sent:
        value = value + z[...].astype(F32)
    put(value, made, out, lanes, sem)


def exchange(value, axis, distance):
    size = lax.axis_size(axis)
    return lax.ppermute(value, axis, [(i, i ^ distance) for i in range(size)])


def subsets(spans):
    choices = [[]]
    for span in spans:
        choices = choices + [c + [span] for c in choices]
    return choices[1:]


def hop(value, moves):
    tiles, groups = lax.axis_size("tile"), lax.axis_size("tm")
    flip = sum(d * groups if axis == "tile" else d for axis, d in moves)
    return lax.ppermute(
        value, ("tile", "tm"), [(i, i ^ flip) for i in range(tiles * groups)]
    )


def everywhere(value, sent):
    spans = [
        (axis, 1 << n)
        for axis in ("tm", "tile")
        for n in range(lax.axis_size(axis).bit_length() - 1)
    ]
    *terms, last = [hop(sent, moves) for moves in subsets(spans[:2])]
    for start in range(2, len(spans), 2):
        for term in terms + [last]:
            value = value + term.astype(F32)
        sent = value.astype(BF16)
        *terms, last = [hop(sent, moves) for moves in subsets(spans[start : start + 2])]
    for term in terms:
        value = value + term.astype(F32)
    return value, last


def outside(*values):
    return [pltpu.with_memory_space_constraint(x, pltpu.HBM) for x in values]


def inside(*values):
    return [pltpu.with_memory_space_constraint(x, pltpu.VMEM) for x in values]


def per_device(
    probes,
    footprints,
    owner_tile,
    sounding_index,
    flux_step,
    entry_count,
    departure,
    live_count,
    error_id,
    precision_table,
    temporal_factor,
    row_factor,
    column_factor,
):
    count, steps, cells = probes.shape
    slots, block_rows = footprints.shape[:2]
    groups = lax.axis_size("tm")
    own_blocks = departure.shape[0]
    blocks = own_blocks * groups * lax.axis_size("tile")
    size = steps * count
    params = pltpu.CompilerParams(vmem_limit_bytes=VMEM_LIMIT)

    peers = [exchange(probes, "tm", d) for d in range(1, groups)]
    held, turned, own, table, rows, mix_f, mix_b, unmix_b, wide_f, wide_b, base, place, step_of = (
        pl.pallas_call(
            functools.partial(prepare_kernel, groups, steps, count, blocks, own_blocks),
            out_shape=[
                pltpu.VMEM((slots * block_rows, cells), BF16),
                pltpu.VMEM((cells, slots * block_rows), BF16),
                pltpu.VMEM(probes.shape, BF16),
                pltpu.VMEM(precision_table.shape, F32),
                pltpu.SMEM(row_factor.shape, F32),
                pltpu.VMEM((2 * size, groups * size), BF16),
                pltpu.VMEM((2 * size, groups * size), BF16),
                pltpu.VMEM((groups, 2 * size, 2 * size), BF16),
                pltpu.VMEM((2 * LANES, 2 * LANES), BF16),
                pltpu.VMEM((2 * LANES, 2 * LANES), BF16),
                pltpu.VMEM((blocks * (count + 2), block_rows), F32),
                pltpu.SMEM((slots,), jnp.int32),
                pltpu.SMEM((slots,), jnp.int32),
            ],
            in_specs=[in_hbm] * 11,
            out_specs=[in_vmem] * 4 + [in_smem] + [in_vmem] * 6 + [in_smem] * 2,
            scratch_shapes=[
                pltpu.SMEM(temporal_factor.shape, F32),
                pltpu.VMEM(column_factor.shape, F32),
                pltpu.SMEM((slots,), jnp.int32),
                pltpu.SMEM((slots,), jnp.int32),
                pltpu.SMEM((slots,), jnp.int32),
                pltpu.VMEM(departure.shape, F32),
                pltpu.SMEM((1 + 2 * own_blocks,), jnp.int32),
                pltpu.SemaphoreType.DMA((10,)),
                pltpu.SemaphoreType.DMA((slots,)),
            ],
            compiler_params=params,
            name="prepare",
        )(
            *outside(
                footprints.reshape(slots * block_rows, cells), probes, precision_table,
                temporal_factor, row_factor, column_factor, owner_tile.reshape(slots),
                sounding_index, flux_step, departure,
            ),
            jnp.concatenate([entry_count, live_count, error_id]),
        )
    )
    held, turned, own, table, mix_f, mix_b, unmix_b, wide_f, wide_b, base = inside(
        held, turned, own, table, mix_f, mix_b, unmix_b, wide_f, wide_b, base
    )

    total, sent = pl.pallas_call(
        functools.partial(predict_kernel, groups, steps, count),
        out_shape=[
            jax.ShapeDtypeStruct(base.shape, F32),
            jax.ShapeDtypeStruct(base.shape, BF16),
        ],
        in_specs=[in_vmem] * (groups + 1) + [in_smem] + [in_vmem] * 3 + [in_smem] * 2,
        out_specs=[in_vmem] * 2,
        scratch_shapes=[
            pltpu.VMEM((size, cells), F32),
            pltpu.VMEM((size, cells), BF16),
        ],
        compiler_params=params,
        name="predict",
    )(own, *peers, mix_f, rows, wide_f, turned, base, place, step_of)
    near, far = everywhere(total, sent)

    half = cells // 2
    low, adjoint = pl.pallas_call(
        functools.partial(adjoint_kernel, steps, count, blocks),
        out_shape=[
            jax.ShapeDtypeStruct((size, half), BF16),
            jax.ShapeDtypeStruct((size, cells), F32),
        ],
        in_specs=[in_vmem] * 3 + [in_smem] + [in_vmem] * 2 + [in_smem] * 2,
        out_specs=[in_vmem] * 2,
        scratch_shapes=[
            pltpu.VMEM((size, slots * block_rows), BF16),
            pltpu.VMEM((2 * blocks, block_rows), F32),
        ],
        compiler_params=params,
        name="adjoint",
    )(near, far, table, rows, wide_b, held, place, step_of)
    lows = [low] + [exchange(low, "tm", d) for d in range(1, groups)]
    *sent, stacked = pl.pallas_call(
        functools.partial(adjoint_rest_kernel, half // LANES),
        out_shape=[jax.ShapeDtypeStruct((size, half), BF16)] * (groups - 1)
        + [jax.ShapeDtypeStruct((size, half), BF16)],
        in_specs=[in_vmem, in_smem, in_vmem, in_vmem],
        out_specs=[in_vmem] * groups,
        compiler_params=params,
        name="adjoint_rest",
    )(adjoint, rows, wide_b, unmix_b)
    highs = [exchange(z, "tm", d + 1) for d, z in enumerate(sent)]
    low_lanes, high_lanes = slice(0, half), slice(half, cells)
    high = pl.pallas_call(
        functools.partial(own_kernel, high_lanes),
        out_shape=jax.ShapeDtypeStruct((size, half), F32),
        in_specs=[in_vmem] * 3,
        out_specs=in_vmem,
        compiler_params=params,
        name="own",
    )(own, stacked, unmix_b)
    scratch = [pltpu.VMEM((count, steps, half), BF16), pltpu.SemaphoreType.DMA]
    made = pl.pallas_call(
        functools.partial(finish_low_kernel, groups, low_lanes),
        out_shape=jax.ShapeDtypeStruct(probes.shape, BF16),
        in_specs=[in_vmem] * (groups + 2),
        out_specs=in_hbm,
        scratch_shapes=scratch,
        compiler_params=params,
        name="finish_low",
    )(*lows, own, mix_b)
    return pl.pallas_call(
        functools.partial(finish_high_kernel, high_lanes),
        out_shape=jax.ShapeDtypeStruct(probes.shape, BF16),
        in_specs=[in_vmem] * groups + [in_hbm],
        out_specs=in_hbm,
        input_output_aliases={groups: 0},
        scratch_shapes=scratch,
        compiler_params=params,
        name="finish_high",
    )(high, *highs, made)


def solution(mesh):
    placed = (
        P(("parts", "rep"), "tm", "tile"),
        P(("parts", "tile", "tm"), None, None),
        P(("parts", "tile", "tm"), None),
        P(("parts", "tile", "tm")),
        P(("parts", "tile", "tm")),
        P(("parts", "tile", "tm")),
        P(("parts", "tile", "tm"), None),
        P(("parts", "tile", "tm")),
        P(("parts", "tile", "tm")),
        P(),
        P(),
        P(),
        P(),
    )
    return jax.shard_map(
        per_device,
        mesh=mesh,
        in_specs=placed,
        out_specs=P(("parts", "rep"), "tm", "tile"),
        check_vma=False,
    )
```
